128 devices in a mesh: space: 16 (over y_hi, x, core), tm: 8 (over z, y_lo).
Axes of the slice: x: 4, y: 4 (y_hi: 2, y_lo: 2; y = y_hi * 2 + y_lo), z: 4, core: 2. Of those that a mesh axis runs over, the one named last changes fastest.
Arguments:
- series: bfloat16 [16384, 2, 512], P('space', None, 'tm'), may hold values from -6 to 6
- space_basis: bfloat16 [16384, 16384], P('space', 'tm'), may hold values from -0.046875 to 0.046875
- time_basis: bfloat16 [512, 512], P('tm'), may hold values from -0.25 to 0.25
- space_eig: float32 [16384], replicated, may hold values from 0.3 to 3
- time_eig: float32 [512], replicated, may hold values from 0.3 to 3
Outputs:
- alpha: bfloat16 [16384, 2, 512], P('space', None, 'tm')
- grad_space: bfloat16 [16384, 16, 1024], P('space', None, 'tm')
The draws below stay inside these ranges and needn't reach their ends.
All inputs are finite; a program needn't handle non-finite values.
Results may differ from the reference program's by a relative error of at most 0.0063.
Values may be sent and summed in bfloat16 or wider, within the bound.
No kernel may reach another device: no remote copies, remote signals or barrier semaphores. Data moves between devices by JAX's collectives and lax.ppermute only.
A program may use at most 64 MiB of HBM per device.

```python
import math
import jax
import jax.numpy as jnp

STATIONS = 16384
TIMES = 512
REPS = 2
N_SPACE = 16


def steps_of(stream_key, shape, cuts, smallest, high):
    level, own = 1.0, jax.random.fold_in(stream_key, 6)
    for dim, blocks in cuts:
        heights = jnp.exp(jax.random.uniform(jax.random.fold_in(own, dim), (blocks,), jnp.float32, smallest / len(cuts), high / len(cuts)))
        level = level * jnp.repeat(heights, shape[dim] // blocks).reshape([-1 if axis == dim else 1 for axis in range(len(shape))])
    return level


def bell_draw(stream_key, extent, spread, reach, split=(), held_as=jnp.bfloat16):
    entries = jax.random.normal(stream_key, extent, jnp.float32) * spread
    if len(split) > 0:
        entries = steps_of(stream_key, extent, split, -0.22, 0.18) * entries
    return jnp.clip(entries, min=-reach, max=reach).astype(held_as)


def setup_inputs(seed: int = 0) -> dict:
    splits = jax.random.split(jax.random.key(seed), 6)
    return {
        "series": bell_draw(splits[0], (STATIONS, REPS, TIMES), 1.0, 6.0, ((0, 16), (2, 8))),
        "space_basis": bell_draw(splits[1], (STATIONS, STATIONS), STATIONS ** -0.5, 0.046875, ((0, 16), (1, 8))),
        "time_basis": bell_draw(splits[2], (TIMES, TIMES), TIMES ** -0.5, 0.25, ((0, 8),)),
        "space_eig": jnp.clip(jnp.exp(jax.random.uniform(splits[3], (STATIONS,), jnp.float32, math.log(0.3), math.log(3.0))), 0.3, 3.0),
        "time_eig": jnp.clip(jnp.exp(jax.random.uniform(splits[4], (TIMES,), jnp.float32, math.log(0.3), math.log(3.0))), 0.3, 3.0),
    }


def reference(series, space_basis, time_basis, space_eig, time_eig):
    flat = series.reshape(STATIONS * REPS, TIMES)
    rotated = jnp.dot(flat, time_basis, preferred_element_type=jnp.float32).astype(jnp.bfloat16)
    rotated = rotated.reshape(STATIONS, REPS * TIMES)
    spectral = jnp.dot(space_basis.T, rotated, preferred_element_type=jnp.float32)
    denom = space_eig[:, None, None] * time_eig[None, None, :] + 0.1
    scaled_spec = (spectral.reshape(STATIONS, REPS, TIMES) / denom).astype(jnp.bfloat16)
    scaled_spec = scaled_spec.reshape(STATIONS, REPS * TIMES)
    back = jnp.dot(space_basis, scaled_spec, preferred_element_type=jnp.float32).astype(jnp.bfloat16)
    alpha = jnp.dot(back.reshape(STATIONS * REPS, TIMES), time_basis.T, preferred_element_type=jnp.float32)
    alpha = alpha.astype(jnp.bfloat16).reshape(STATIONS, REPS, TIMES)
    weighted = back.reshape(STATIONS, REPS, TIMES).astype(jnp.float32) * time_eig[None, None, :]
    weighted = (weighted / (REPS * TIMES)).astype(jnp.bfloat16).reshape(STATIONS, REPS * TIMES)
    grad = jnp.dot(weighted, back.T, preferred_element_type=jnp.float32).astype(jnp.bfloat16)
    return alpha, grad.reshape(STATIONS, N_SPACE, STATIONS // N_SPACE)
```

```python
import functools

import jax
import jax.numpy as jnp
from jax import lax
from jax.experimental import pallas as pl
from jax.experimental.pallas import tpu as pltpu
from jax.sharding import PartitionSpec as P

TIMES = 512
REPS = 2
BF = jnp.bfloat16
F32 = jnp.float32
NT = (((1,), (1,)), ((), ()))
VMEM_LIMIT = 48 * 1024 * 1024


def vmem():
    return pl.BlockSpec(memory_space=pltpu.VMEM)


def params():
    return pltpu.CompilerParams(vmem_limit_bytes=VMEM_LIMIT)


def cost(flops, nbytes):
    return pl.CostEstimate(flops=flops, bytes_accessed=nbytes, transcendentals=0)


def space_pairs(move):
    pairs = []
    for i in range(16):
        yh, x, c = i // 8, (i // 2) % 4, i % 2
        yh, x, c = move(yh, x, c)
        pairs.append((i, yh * 8 + (x % 4) * 2 + c))
    return pairs


def tm_pairs(move):
    pairs = []
    for i in range(8):
        z, yl = move(i // 2, i % 2)
        pairs.append((i, (z % 4) * 2 + yl))
    return pairs


X_UP = ("space", space_pairs(lambda yh, x, c: (yh, x + 1, c)))
X_DOWN = ("space", space_pairs(lambda yh, x, c: (yh, x - 1, c)))
Y_HI = ("space", space_pairs(lambda yh, x, c: (1 - yh, x, c)))
CORE = ("space", space_pairs(lambda yh, x, c: (yh, x, 1 - c)))
Z_UP = ("tm", tm_pairs(lambda z, yl: (z + 1, yl)))
Z_DOWN = ("tm", tm_pairs(lambda z, yl: (z - 1, yl)))
Y_LO = ("tm", tm_pairs(lambda z, yl: (z, 1 - yl)))


def send(v, route):
    return lax.ppermute(v, route[0], route[1])


def ring_gather(pair, up, down):
    half = pair.shape[0] // 2
    below = send(pair, up)
    above = send(pair, down)
    far_top = send(below[:half], up)
    far_bot = send(above[half:], down)
    return pair, below, above, far_top, far_bot


def rotate_kernel(n_ser, *refs):
    first = refs[:5]
    ser = refs[5:10] if n_ser else first
    out_ref, tb0, tb1 = refs[-3:]
    half = 512

    def shards(group, size):
        p, b, a, ft, fb = group
        return [(p, 0), (p, size), (b, 0), (b, size), (a, 0), (a, size), (ft, 0), (fb, 0)]

    tb0[...] = jnp.zeros_like(tb0)
    tb1[...] = jnp.zeros_like(tb1)
    for k, (ref, base) in enumerate(shards(first, 768)):
        for c in range(4):
            block = ref[base + 512 + 64 * c : base + 512 + 64 * (c + 1), :]
            tb0[k * 128 : k * 128 + 64, c * 128 : (c + 1) * 128] = block
            tb1[k * 128 + 64 : k * 128 + 128, c * 128 : (c + 1) * 128] = block
    size = 512 if n_ser else 768
    wide = jnp.concatenate([ref[base : base + half, :] for ref, base in shards(ser, size)], axis=1)
    for h, tb in enumerate((tb0, tb1)):
        part = jnp.dot(wide, tb[...], preferred_element_type=F32)
        out_ref[:, h * half : (h + 1) * half] = part.T.astype(BF)


def rotate(first, ser):
    args = list(first) + (list(ser) if ser is not None else [])
    return pl.pallas_call(
        functools.partial(rotate_kernel, 5 if ser is not None else 0),
        out_shape=jax.ShapeDtypeStruct((512, 1024), BF),
        in_specs=[vmem()] * len(args),
        out_specs=vmem(),
        scratch_shapes=[pltpu.VMEM((1024, 512), BF), pltpu.VMEM((1024, 512), BF)],
        compiler_params=params(),
        cost_estimate=cost(2 * 1024 * 1024 * 512, 4 << 20),
        name="rotate",
    )(*args)


def spectral_partner(idx, xt, basis):
    u, rows = xt.shape

    def kernel(idx_ref, x_ref, a_ref, o_ref):
        o_ref[...] = jnp.dot(x_ref[...], a_ref[...], preferred_element_type=F32).astype(BF)

    return pl.pallas_call(
        kernel,
        out_shape=jax.ShapeDtypeStruct((u, 1024), BF),
        grid_spec=pltpu.PrefetchScalarGridSpec(
            num_scalar_prefetch=1,
            grid=(4,),
            in_specs=[
                pl.BlockSpec((u, rows), lambda m, i: (0, 0)),
                pl.BlockSpec((rows, 256), lambda m, i: (0, i[m])),
            ],
            out_specs=pl.BlockSpec((u, 256), lambda m, i: (0, m)),
        ),
        compiler_params=params(),
        cost_estimate=cost(2 * u * rows * 1024, 4 << 20),
        name="spectral_partner",
    )(idx, xt, basis)


def spectral_far(idx, xt, basis, recv):
    u, rows = xt.shape
    half = u // 2

    def kernel(idx_ref, x_ref, a_ref, r_ref, top_ref, bot_ref):
        y = jnp.dot(x_ref[...], a_ref[...], preferred_element_type=F32) + r_ref[...].astype(F32)
        top_ref[...] = y[:half].astype(BF)
        bot_ref[...] = y[half:].astype(BF)

    return pl.pallas_call(
        kernel,
        out_shape=[jax.ShapeDtypeStruct((half, 256), BF)] * 2,
        grid_spec=pltpu.PrefetchScalarGridSpec(
            num_scalar_prefetch=1,
            grid=(1,),
            in_specs=[
                pl.BlockSpec((u, rows), lambda m, i: (0, 0)),
                pl.BlockSpec((rows, 256), lambda m, i: (0, i[2])),
                pl.BlockSpec((u, 256), lambda m, i: (0, 2)),
            ],
            out_specs=[pl.BlockSpec((half, 256), lambda m, i: (0, 0))] * 2,
        ),
        compiler_params=params(),
        cost_estimate=cost(2 * u * rows * 256, 2 << 20),
        name="spectral_far",
    )(idx, xt, basis, recv)


def spectral_near(idx, xt, basis, recv, from_below, from_above):
    u, rows = xt.shape
    half = u // 2

    def kernel(idx_ref, x_ref, a_ref, r_ref, below_ref, above_ref, own_ref, up_ref, down_ref):
        step = pl.program_id(0)
        y = jnp.dot(x_ref[...], a_ref[...], preferred_element_type=F32) + r_ref[...].astype(F32)

        @pl.when(step == 0)
        def _():
            up_ref[:half] = (y[:half] + below_ref[...].astype(F32)).astype(BF)
            up_ref[half:] = y[half:].astype(BF)

        @pl.when(step == 1)
        def _():
            down_ref[:half] = y[:half].astype(BF)
            down_ref[half:] = (y[half:] + above_ref[...].astype(F32)).astype(BF)

        @pl.when(step == 2)
        def _():
            own_ref[...] = y

    def block(m):
        return jnp.where(m == 0, 1, jnp.where(m == 1, 3, 0))

    return pl.pallas_call(
        kernel,
        out_shape=[
            jax.ShapeDtypeStruct((u, 256), F32),
            jax.ShapeDtypeStruct((u, 256), BF),
            jax.ShapeDtypeStruct((u, 256), BF),
        ],
        grid_spec=pltpu.PrefetchScalarGridSpec(
            num_scalar_prefetch=1,
            grid=(3,),
            in_specs=[
                pl.BlockSpec((u, rows), lambda m, i: (0, 0)),
                pl.BlockSpec((rows, 256), lambda m, i: (0, i[block(m)])),
                pl.BlockSpec((u, 256), lambda m, i: (0, block(m))),
                pl.BlockSpec((half, 256), lambda m, i: (0, 0)),
                pl.BlockSpec((half, 256), lambda m, i: (0, 0)),
            ],
            out_specs=[pl.BlockSpec((u, 256), lambda m, i: (0, 0))] * 3,
        ),
        compiler_params=params(),
        cost_estimate=cost(2 * u * rows * 768, 4 << 20),
        name="spectral_near",
    )(idx, xt, basis, recv, from_below, from_above)


def assemble(col_ref, refs, s_ref):
    pair, below, above, ft, fb, o_near, o_far = refs
    u = pair.shape[0]
    half = u // 2

    def cols(k):
        return pl.ds(pl.multiple_of(col_ref[k] * 256, 256), 256)

    s_ref[:, cols(0)] = pair[...]
    s_ref[:, cols(3)] = below[...]
    s_ref[:, cols(1)] = above[...]
    s_ref[:half, cols(2)] = ft[...]
    s_ref[half:, cols(2)] = fb[...]
    s_ref[:, cols(4)] = o_near[0:u]
    s_ref[:, cols(7)] = o_near[u : 2 * u]
    s_ref[:, cols(5)] = o_near[2 * u : 3 * u]
    s_ref[:, cols(6)] = o_far[...]


def back_far(row_idx, col_idx, basis, shards):
    u = shards[0].shape[0]

    def kernel(row_ref, col_ref, a_ref, *refs):
        s_ref = refs[-1]
        top_ref, bot_ref = refs[-3:-1]
        assemble(col_ref, refs[:7], s_ref)
        y = lax.dot_general(a_ref[...], s_ref[...], NT, preferred_element_type=F32)
        top_ref[...] = y[:128].astype(BF)
        bot_ref[...] = y[128:].astype(BF)

    return pl.pallas_call(
        kernel,
        out_shape=[jax.ShapeDtypeStruct((128, u), BF)] * 2,
        grid_spec=pltpu.PrefetchScalarGridSpec(
            num_scalar_prefetch=2,
            grid=(1,),
            in_specs=[pl.BlockSpec((256, 2048), lambda m, r, c: (r[2], 0))]
            + [pl.BlockSpec(s.shape, lambda m, r, c: (0, 0)) for s in shards],
            out_specs=[pl.BlockSpec((128, u), lambda m, r, c: (0, 0))] * 2,
            scratch_shapes=[pltpu.VMEM((u, 2048), BF)],
        ),
        compiler_params=params(),
        cost_estimate=cost(2 * u * 2048 * 256, 3 << 20),
        name="back_far",
    )(row_idx, col_idx, basis, *shards)


def back_near(row_idx, col_idx, basis, shards, from_below, from_above):
    u = shards[0].shape[0]

    def kernel(row_ref, col_ref, a_ref, *refs):
        below_ref, above_ref, own_ref, up_ref, down_ref, s_ref = refs[-6:]
        step = pl.program_id(0)

        @pl.when(step == 0)
        def _():
            assemble(col_ref, refs[:7], s_ref)

        y = lax.dot_general(a_ref[...], s_ref[...], NT, preferred_element_type=F32)

        @pl.when(step == 0)
        def _():
            up_ref[:128] = (y[:128] + below_ref[...].astype(F32)).astype(BF)
            up_ref[128:] = y[128:].astype(BF)

        @pl.when(step == 1)
        def _():
            down_ref[:128] = y[:128].astype(BF)
            down_ref[128:] = (y[128:] + above_ref[...].astype(F32)).astype(BF)

        @pl.when(step == 2)
        def _():
            own_ref[...] = y

    def block(m):
        return jnp.where(m == 0, 1, jnp.where(m == 1, 3, 0))

    return pl.pallas_call(
        kernel,
        out_shape=[
            jax.ShapeDtypeStruct((256, u), F32),
            jax.ShapeDtypeStruct((256, u), BF),
            jax.ShapeDtypeStruct((256, u), BF),
        ],
        grid_spec=pltpu.PrefetchScalarGridSpec(
            num_scalar_prefetch=2,
            grid=(3,),
            in_specs=[pl.BlockSpec((256, 2048), lambda m, r, c: (r[block(m)], 0))]
            + [pl.BlockSpec(s.shape, lambda m, r, c: (0, 0)) for s in shards]
            + [pl.BlockSpec((128, u), lambda m, r, c: (0, 0))] * 2,
            out_specs=[pl.BlockSpec((256, u), lambda m, r, c: (0, 0))] * 3,
            scratch_shapes=[pltpu.VMEM((u, 2048), BF)],
        ),
        compiler_params=params(),
        cost_estimate=cost(2 * u * 2048 * 768, 5 << 20),
        name="back_near",
    )(row_idx, col_idx, basis, *shards, from_below, from_above)


def gradient(row_idx, blk_idx, time_row, time_basis, rows, cols):
    flat = [v for q in range(REPS) for v in list(rows[q]) + list(cols[q])]

    def kernel(row_ref, blk_ref, te_ref, tb_ref, *refs):
        ins, (grad_ref, alpha_ref, r_scr, c_scr) = refs[:-4], refs[-4:]
        step = pl.program_id(0)

        @pl.when(step == 0)
        def _():
            for q in range(REPS):
                pair, below, above, ft, fb = ins[12 * q : 12 * q + 5]
                lanes = slice(512 * q, 512 * (q + 1))

                def put(scr, index, size, value):
                    scr[pl.ds(pl.multiple_of(index * size, size), size), lanes] = value

                put(r_scr, row_ref[0], 256, pair[...])
                put(r_scr, row_ref[3], 256, below[...])
                put(r_scr, row_ref[1], 256, above[...])
                put(r_scr, 2 * row_ref[2], 128, ft[...])
                put(r_scr, 2 * row_ref[2] + 1, 128, fb[...])
                pair, below, above, ft, fb, near, far = ins[12 * q + 5 : 12 * q + 12]
                for yh in range(2):
                    part = slice(128 * yh, 128 * (yh + 1))
                    put(c_scr, 8 * yh + blk_ref[0], 128, pair[part, :])
                    put(c_scr, 8 * yh + blk_ref[3], 128, below[part, :])
                    put(c_scr, 8 * yh + blk_ref[1], 128, above[part, :])
                    put(c_scr, 8 * yh + blk_ref[2], 128, (ft, fb)[yh][...])
                    put(c_scr, 8 * yh + blk_ref[4], 128, near[128 * yh : 128 * (yh + 1), :])
                    put(c_scr, 8 * yh + blk_ref[7], 128, near[256 + 128 * yh : 256 + 128 * (yh + 1), :])
                    put(c_scr, 8 * yh + blk_ref[5], 128, near[512 + 128 * yh : 512 + 128 * (yh + 1), :])
                    put(c_scr, 8 * yh + blk_ref[6], 128, far[part, :])

        b = r_scr[pl.ds(pl.multiple_of(step * 256, 256), 256), :]
        w = (b.astype(F32) * te_ref[...] / (REPS * TIMES)).astype(BF)
        g = lax.dot_general(w, c_scr[...], NT, preferred_element_type=F32)
        for a in range(16):
            grad_ref[:, a, :] = g[:, 128 * a : 128 * (a + 1)].astype(BF)
        for q in range(REPS):
            al = lax.dot_general(b[:, 512 * q : 512 * (q + 1)], tb_ref[...], NT, preferred_element_type=F32)
            alpha_ref[:, q, :] = al.astype(BF)

    return pl.pallas_call(
        kernel,
        out_shape=[
            jax.ShapeDtypeStruct((1024, REPS, 64), BF),
            jax.ShapeDtypeStruct((1024, 16, 128), BF),
        ][::-1],
        grid_spec=pltpu.PrefetchScalarGridSpec(
            num_scalar_prefetch=2,
            grid=(4,),
            in_specs=[
                pl.BlockSpec((1, REPS * TIMES), lambda m, r, c: (0, 0)),
                pl.BlockSpec((64, TIMES), lambda m, r, c: (0, 0)),
            ]
            + [pl.BlockSpec(v.shape, lambda m, r, c: (0, 0)) for v in flat],
            out_specs=[
                pl.BlockSpec((256, 16, 128), lambda m, r, c: (m, 0, 0)),
                pl.BlockSpec((256, REPS, 64), lambda m, r, c: (m, 0, 0)),
            ],
            scratch_shapes=[pltpu.VMEM((1024, REPS * TIMES), BF), pltpu.VMEM((2048, REPS * TIMES), BF)],
        ),
        compiler_params=params(),
        cost_estimate=cost(2 * 1024 * 1024 * 2048, 14 << 20),
        name="gradient",
    )(row_idx, blk_idx, time_row, time_basis, *flat)


def ordered_pair(own, other, position, axis):
    first = jnp.where(position == 0, own, other)
    second = jnp.where(position == 0, other, own)
    return jnp.concatenate([first, second], axis=axis)


def per_device(series, space_basis, time_basis, space_eig, time_eig):
    space, tm = lax.axis_index("space"), lax.axis_index("tm")
    yh, x, core = space // 8, (space // 2) % 4, space % 2
    z, yl = tm // 2, tm % 2
    ring = jnp.arange(4, dtype=jnp.int32)
    x_ring, z_ring = (x + ring) % 4, (z + ring) % 4
    col_own, col_other = core * 4 + x_ring, (1 - core) * 4 + x_ring
    col_idx = jnp.concatenate([col_own, col_other]).astype(jnp.int32)
    blk_idx = jnp.concatenate([x_ring * 2 + core, x_ring * 2 + 1 - core]).astype(jnp.int32)
    row_idx = z_ring.astype(jnp.int32)
    own_cols = tm * 2048 + core * 1024 + x * 256 + yh * 128
    eig_own = lax.dynamic_slice_in_dim(space_eig, own_cols, 128)
    denom = time_eig[:, None] * eig_own[None, :] + 0.1
    time_row = jnp.tile(time_eig, REPS)[None, :]

    packs = [jnp.concatenate([series[:512, q], series[512:, q]], axis=1) for q in range(REPS)]
    tb_pack = jnp.concatenate([time_basis[:, 128 * c : 128 * (c + 1)] for c in range(4)], axis=0)
    packs[0] = jnp.concatenate([packs[0], tb_pack], axis=0)
    gathered = []
    for q in range(REPS):
        pair = jnp.concatenate([packs[q], send(packs[q], Y_LO)], axis=0)
        gathered.append(ring_gather(pair, Z_UP, Z_DOWN))

    rows, cols = [], []
    for q in range(REPS):
        with jax.named_scope("rotation"):
            xt = rotate(gathered[0], gathered[q] if q else None)
        with jax.named_scope("spectral"):
            recv = send(spectral_partner(col_other, xt, space_basis), CORE)
            top, bot = spectral_far(col_own, xt, space_basis, recv)
            own, up, down = spectral_near(
                col_own, xt, space_basis, recv, send(top, X_UP), send(bot, X_DOWN)
            )
            total = own + send(up, X_UP).astype(F32) + send(down, X_DOWN).astype(F32)
            mine = lax.dynamic_slice_in_dim(total, yh * 128, 128, 1)
            theirs = lax.dynamic_slice_in_dim(total, (1 - yh) * 128, 128, 1).astype(BF)
            spectral = mine + send(theirs, Y_HI).astype(F32)
            scaled = (spectral / denom).astype(BF)
        with jax.named_scope("scaled_gather"):
            pair = ordered_pair(scaled, send(scaled, Y_HI), yh, 1)
            shards = ring_gather(pair, X_UP, X_DOWN)
            near = send(jnp.concatenate(shards[:3], axis=0), CORE)
            far = send(jnp.concatenate(shards[3:], axis=0), CORE)
            shards = shards + (near, far)
        with jax.named_scope("back"):
            top, bot = back_far(row_idx, col_idx, space_basis, shards)
            own, up, down = back_near(
                row_idx, col_idx, space_basis, shards, send(top, Z_UP), send(bot, Z_DOWN)
            )
            total = own + send(up, Z_UP).astype(F32) + send(down, Z_DOWN).astype(F32)
            mine = lax.dynamic_slice_in_dim(total, yl * 128, 128, 0)
            theirs = lax.dynamic_slice_in_dim(total, (1 - yl) * 128, 128, 0).astype(BF)
            back = (mine + send(theirs, Y_LO).astype(F32)).astype(BF)
        with jax.named_scope("back_gather"):
            pair = ordered_pair(back, send(back, Y_LO), yl, 0)
            rows.append(ring_gather(pair, Z_UP, Z_DOWN))
            pair = ordered_pair(back, send(back, Y_HI), yh, 0)
            shards = ring_gather(pair, X_UP, X_DOWN)
            near = send(jnp.concatenate(shards[:3], axis=0), CORE)
            far = send(jnp.concatenate(shards[3:], axis=0), CORE)
            cols.append(shards + (near, far))
    with jax.named_scope("gradient"):
        grad, alpha = gradient(row_idx, blk_idx, time_row, time_basis, rows, cols)
    return alpha, grad


def solution(mesh):
    return jax.shard_map(
        per_device,
        mesh=mesh,
        in_specs=(P("space", None, "tm"), P("space", "tm"), P("tm", None), P(), P()),
        out_specs=(P("space", None, "tm"), P("space", None, "tm")),
        check_vma=False,
    )
```

```python
import functools

import jax
import jax.numpy as jnp
from jax import lax
from jax.experimental import pallas as pl
from jax.experimental.pallas import tpu as pltpu
from jax.sharding import PartitionSpec as P

TIMES = 512
REPS = 2
CHUNKS = 1
U = TIMES // CHUNKS
H = U // 2
PARTS = 2
BF = jnp.bfloat16
F32 = jnp.float32
NT = (((1,), (1,)), ((), ()))
AXES = ("space", "tm")


def vmem():
    return pl.BlockSpec(memory_space=pltpu.VMEM)


def params(mib):
    return pltpu.CompilerParams(vmem_limit_bytes=mib * 1024 * 1024)


def cost(flops, nbytes):
    return pl.CostEstimate(flops=flops, bytes_accessed=nbytes, transcendentals=0)


def route(move):
    pairs = []
    for i in range(128):
        s, t = i // 8, i % 8
        yh, x, c, z, yl = move(s // 8, (s // 2) % 4, s % 2, t // 2, t % 2)
        pairs.append((i, (yh * 8 + (x % 4) * 2 + c) * 8 + (z % 4) * 2 + yl))
    return pairs


X_RING = route(lambda yh, x, c, z, yl: (yh, x + 1 - 2 * c, c, z, yl))
Z_RING = route(lambda yh, x, c, z, yl: (yh, x, c, z + 1 - 2 * c, yl))
X_UP = route(lambda yh, x, c, z, yl: (yh, x + 1, c, z, yl))
X_DOWN = route(lambda yh, x, c, z, yl: (yh, x - 1, c, z, yl))
Z_UP = route(lambda yh, x, c, z, yl: (yh, x, c, z + 1, yl))
Z_DOWN = route(lambda yh, x, c, z, yl: (yh, x, c, z - 1, yl))
Y_HI = route(lambda yh, x, c, z, yl: (1 - yh, x, c, z, yl))
Y_LO = route(lambda yh, x, c, z, yl: (yh, x, c, z, 1 - yl))
CORE = route(lambda yh, x, c, z, yl: (yh, x, 1 - c, z, yl))


def send(v, pairs):
    return lax.ppermute(v, AXES, pairs)


def split(v, parts):
    rows = v.shape[0] // parts
    return [v[rows * i : rows * (i + 1)] for i in range(parts)]


def gather(piece, swap, ring, parts, late=0):
    own = split(piece, parts)
    rounds = parts - late
    other = [send(v, swap) for v in own[:rounds]] if late else split(send(piece, swap), parts)
    hops = []
    for hop in range(4):
        if hop:
            own = [send(v, ring) for v in own]
            other = [send(v, ring) for v in other]
        hops += [own, other + [send(v, swap) for v in own[rounds:]]]
    return hops


def after(v, *others):
    return lax.optimization_barrier((v, *others))[0]


def ring_gather(pieces, ring):
    hops = list(pieces)
    for _ in range(3):
        pieces = [[send(v, ring) for v in parts] for parts in pieces]
        hops += pieces
    return hops


def gather_both(own, other):
    z = [jnp.concatenate([own, other], axis=0)]
    across = send(own, Y_HI)
    first = send(own, X_RING)
    z.append(send(z[0], Z_RING))
    x = [own, jnp.concatenate([across, first], axis=0)]
    x.append(send(after(x[1], z[1]), X_RING))
    z.append(send(z[1], Z_RING))
    x.append(send(after(x[2], z[2]), X_RING))
    z.append(send(z[2], Z_RING))
    x.append(send(after(x[3][:128], z[3]), X_RING))
    return z, x + [send(v, CORE) for v in x]


def ring_reduce(blocks, operand, up, down, swap):
    far = blocks(operand, (2,))
    near = blocks(operand, (1, 3))
    got = []
    for half in (1, 0):
        top, bot = split(far[half][0], 2)
        below, above = send(top, up), send(bot, down)
        to_up, to_down = split(near[half][0], 2), split(near[half][1], 2)
        to_up = [(to_up[0] + below.astype(F32)).astype(BF), to_up[1].astype(BF)]
        to_down = [to_down[0].astype(BF), (to_down[1] + above.astype(F32)).astype(BF)]
        to_up, to_down = jnp.concatenate(to_up, axis=0), jnp.concatenate(to_down, axis=0)
        if half:
            to_up, to_down, operand = lax.optimization_barrier((to_up, to_down, operand))
        got.append((send(to_up, up), send(to_down, down)))
    own = blocks(operand, (0,))
    away, kept = [own[h][0] + u.astype(F32) + d.astype(F32) for h, (u, d) in zip((1, 0), got)]
    to_kept, to_away = lax.optimization_barrier((send(away.astype(BF), swap), send(kept.astype(BF), swap)))
    return kept + to_kept.astype(F32), away + to_away.astype(F32)


def hop_at(hops, step):
    return jnp.where(step == 0, hops[0], hops[-1])


def rotate(pos, pieces):
    def kernel(pos_ref, *refs):
        ins, (out_ref, tb_ref, ser_ref) = refs[:-3], refs[-3:]
        for k in range(8):
            for p in range(2):
                ref = ins[2 * k + p]
                at = 64 * k + 32 * p
                tb_ref[at : at + 16] = ref[64:80, :512]
                tb_ref[at + 16 : at + 32] = ref[64:80, 512:]
                ser_ref[64 * k : 64 * (k + 1), 1024 * p : 1024 * (p + 1)] = ref[:64, :]
        tb = tb_ref[...].T
        yh = pos_ref[0]
        for p in range(2):
            cols = slice(1024 * p, 1024 * (p + 1))
            part = jnp.dot(tb, ser_ref[:, cols], preferred_element_type=F32).astype(BF)
            for j in range(2 * CHUNKS):
                half = jnp.where(yh == 0, j % 2, 1 - j % 2)
                row = pl.multiple_of((j // 2) * U + half * H, H)
                out_ref[pl.ds(row, H), cols] = part[j * H : (j + 1) * H]

    return pl.pallas_call(
        kernel,
        out_shape=jax.ShapeDtypeStruct((TIMES, 2048), BF),
        in_specs=[pl.BlockSpec(memory_space=pltpu.SMEM)] + [vmem()] * 16,
        out_specs=vmem(),
        scratch_shapes=[pltpu.VMEM((TIMES, TIMES), BF), pltpu.VMEM((TIMES, 2048), BF)],
        compiler_params=params(48),
        cost_estimate=cost(2 * 512 * 512 * 2048, 6 << 20),
        name="rotate",
    )(pos, *pieces)


def spectral_blocks(idx, chunk, xt, own, partner, hops):
    far = hops[0] == 2
    dtype = BF if far else F32

    def kernel(idx_ref, x_ref, a_ref, b_ref, mine_ref, theirs_ref):
        y = jnp.dot(x_ref[:, :1024], a_ref[...], preferred_element_type=F32)
        y += jnp.dot(x_ref[:, 1024:], b_ref[...], preferred_element_type=F32)
        mine_ref[0] = y[:H].astype(dtype)
        theirs_ref[0] = y[H:].astype(dtype)

    n = len(hops)
    return pl.pallas_call(
        kernel,
        out_shape=[jax.ShapeDtypeStruct((n, H, 512), dtype)] * 2,
        grid_spec=pltpu.PrefetchScalarGridSpec(
            num_scalar_prefetch=1,
            grid=(n,),
            in_specs=[
                pl.BlockSpec((U, 2048), lambda m, i: (chunk, 0)),
                pl.BlockSpec((1024, 512), lambda m, i: (0, i[hop_at(hops, m)])),
                pl.BlockSpec((1024, 512), lambda m, i: (0, i[hop_at(hops, m)])),
            ],
            out_specs=[pl.BlockSpec((1, H, 512), lambda m, i: (m, 0, 0))] * 2,
        ),
        compiler_params=params(48),
        cost_estimate=cost(2 * U * 2048 * 512 * n, (3 << 20) * n),
        name="spectral_far" if far else "spectral_near",
    )(idx, xt, own, partner)


def back_blocks(row_idx, col_idx, pos, own, partner, hops, shards):
    far = hops[0] == 2
    dtype = BF if far else F32
    flat = [v for parts in shards for v in parts]
    rows = flat[0].shape[0]

    def kernel(row_ref, col_ref, pos_ref, a_ref, b_ref, *refs):
        ins, (mine_ref, theirs_ref, s_ref, y_ref) = refs[:-4], refs[-4:]

        @pl.when(pl.program_id(0) == 0)
        def _():
            for k in range(4):
                cols = pl.ds(pl.multiple_of(col_ref[k] * 512, 512), 512)
                per_hop = len(ins) // 4
                for n in range(per_hop):
                    s_ref[rows * n : rows * (n + 1), cols] = ins[per_hop * k + n][...]

        y_ref[:256] = lax.dot_general(a_ref[...], s_ref[...], NT, preferred_element_type=F32)
        y_ref[256:] = lax.dot_general(b_ref[...], s_ref[...], NT, preferred_element_type=F32)
        at = pl.multiple_of(pos_ref[0] * 128, 128)
        off = pl.multiple_of(128 - at, 128)
        mine_ref[0, :128] = y_ref[pl.ds(at, 128)].astype(dtype)
        mine_ref[0, 128:] = y_ref[pl.ds(256 + at, 128)].astype(dtype)
        theirs_ref[0, :128] = y_ref[pl.ds(off, 128)].astype(dtype)
        theirs_ref[0, 128:] = y_ref[pl.ds(256 + off, 128)].astype(dtype)

    n = len(hops)
    return pl.pallas_call(
        kernel,
        out_shape=[jax.ShapeDtypeStruct((n, 256, U), dtype)] * 2,
        grid_spec=pltpu.PrefetchScalarGridSpec(
            num_scalar_prefetch=3,
            grid=(n,),
            in_specs=[pl.BlockSpec((256, 2048), lambda m, r, c, p: (r[hop_at(hops, m)], 0))] * 2
            + [pl.BlockSpec(v.shape, lambda m, r, c, p: (0, 0)) for v in flat],
            out_specs=[pl.BlockSpec((1, 256, U), lambda m, r, c, p: (m, 0, 0))] * 2,
            scratch_shapes=[pltpu.VMEM((U, 2048), BF), pltpu.VMEM((512, U), F32)],
        ),
        compiler_params=params(48),
        cost_estimate=cost(2 * U * 2048 * 512 * n, (3 << 20) * n),
        name="back_far" if far else "back_near",
    )(row_idx, col_idx, pos, own, partner, *flat)


def gradient(row_idx, blk_idx, time_row, time_basis, pieces):
    rows, near = pieces
    flat = rows + near
    wide = REPS * U

    def kernel(row_ref, blk_ref, te_ref, tb_ref, *refs):
        ins, (grad_ref, alpha_ref, r_scr, c_scr, sems) = refs[:-5], refs[-5:]
        step = pl.program_id(0)

        @pl.when(step == 0)
        def _():
            copies = []
            n = 0
            for ref in ins:
                for row in range(0, ref.shape[0], 128):
                    scr, at = (r_scr, row_ref[n]) if n < 8 else (c_scr, blk_ref[n - 8])
                    place = scr.at[pl.ds(pl.multiple_of(at * 128, 128), 128)]
                    copies.append(pltpu.make_async_copy(ref.at[row : row + 128], place, sems.at[n]))
                    n += 1
            for copy in copies:
                copy.start()
            for copy in copies:
                copy.wait()

        b = r_scr[pl.ds(pl.multiple_of(step * 256, 256), 256), :]
        w = (b.astype(F32) * te_ref[...] / (REPS * TIMES)).astype(BF)
        g = lax.dot_general(w, c_scr[...], NT, preferred_element_type=F32)
        grad_ref[...] = g.astype(BF).reshape(256, 16, 128)
        for q in range(REPS):
            al = jnp.zeros((64, 256), F32)
            for k in range(CHUNKS):
                lanes = slice(wide * k + U * q, wide * k + U * (q + 1))
                al += lax.dot_general(tb_ref[:, U * k : U * (k + 1)], b[:, lanes], NT, preferred_element_type=F32)
            alpha_ref[q] = al.astype(BF)

    return pl.pallas_call(
        kernel,
        out_shape=[
            jax.ShapeDtypeStruct((1024, 16, 128), BF),
            jax.ShapeDtypeStruct((REPS, 64, 1024), BF),
        ],
        grid_spec=pltpu.PrefetchScalarGridSpec(
            num_scalar_prefetch=2,
            grid=(4,),
            in_specs=[
                pl.BlockSpec((1, REPS * TIMES), lambda m, r, c: (0, 0)),
                pl.BlockSpec((64, TIMES), lambda m, r, c: (0, 0)),
            ]
            + [pl.BlockSpec(memory_space=pl.ANY)] * len(flat),
            out_specs=[
                pl.BlockSpec((256, 16, 128), lambda m, r, c: (m, 0, 0)),
                pl.BlockSpec((REPS, 64, 256), lambda m, r, c: (0, 0, m)),
            ],
            scratch_shapes=[
                pltpu.VMEM((1024, REPS * TIMES), BF),
                pltpu.VMEM((2048, REPS * TIMES), BF),
                pltpu.SemaphoreType.DMA((24,)),
            ],
        ),
        compiler_params=params(24),
        cost_estimate=cost(2 * 1024 * 1024 * 2048, 14 << 20),
        name="gradient",
    )(row_idx, blk_idx, time_row, time_basis, *flat)


def ordered(own, other, position, axis):
    first = jnp.where(position == 0, own, other)
    second = jnp.where(position == 0, other, own)
    return jnp.concatenate([first, second], axis=axis)


def per_device(series, space_basis, time_basis, space_eig, time_eig):
    space, tm = lax.axis_index("space"), lax.axis_index("tm")
    yh, x, core = space // 8, (space // 2) % 4, space % 2
    z, yl = tm // 2, tm % 2
    sign = 1 - 2 * core
    ring = jnp.arange(4, dtype=jnp.int32)
    x_up, z_up = (x + ring) % 4, (z + ring) % 4
    x_behind, z_behind = (x - sign * ring) % 4, (z - sign * ring) % 4
    y_lo_pos = jnp.stack([yl]).astype(jnp.int32)
    y_hi_pos = jnp.stack([yh]).astype(jnp.int32)
    row_at = jnp.stack([z_behind * 2 + yl, z_behind * 2 + 1 - yl], axis=1).reshape(8).astype(jnp.int32)
    col_at = jnp.stack([yh * 8 + x_behind * 2, (1 - yh) * 8 + x_behind * 2], axis=1).reshape(8)
    blk_at = jnp.concatenate([col_at + core, x_other(col_at, x, sign, yh) + 1 - core]).astype(jnp.int32)
    eig_own = lax.dynamic_slice_in_dim(space_eig, tm * 2048 + x * 512, 512)
    time_row = jnp.concatenate(
        [time_eig[U * k : U * (k + 1)] for k in range(CHUNKS) for _ in range(REPS)]
    )[None, :]

    with jax.named_scope("series_gather"):
        turned = jnp.transpose(series, (1, 2, 0))
        mine = lax.dynamic_index_in_dim(turned, core, 0, keepdims=False)
        theirs = lax.dynamic_index_in_dim(turned, 1 - core, 0, keepdims=False)
        theirs = send(theirs, CORE)
        theirs, basis = lax.optimization_barrier((theirs, space_basis))
        partner = send(basis, CORE)
        packs = [jnp.concatenate([time_basis[32 * p : 32 * p + 16], time_basis[32 * p + 16 : 32 * p + 32]], axis=1) for p in range(2)]
        shard = jnp.concatenate([mine, packs[0], theirs, packs[1]], axis=0)
        pieces = [v for parts in gather(shard, Y_LO, Z_RING, 2, late=1) for v in parts]
    with jax.named_scope("rotation"):
        xt = rotate(y_hi_pos, pieces)

    pieces = []
    for k in range(CHUNKS):
        with jax.named_scope("spectral"):

            def blocks(operand, hops):
                return spectral_blocks(x_up.astype(jnp.int32), k, operand, space_basis, partner, hops)

            spectral = ring_reduce(blocks, xt, X_UP, X_DOWN, Y_HI)
            scaled = []
            for v, half in zip(spectral, (yh, 1 - yh)):
                eig_rows = lax.dynamic_slice_in_dim(time_eig, k * U + half * H, H)
                denom = eig_rows[:, None] * eig_own[None, :] + 0.1
                scaled.append((v / denom).astype(BF))
        with jax.named_scope("scaled_gather"):
            shards = ring_gather([split(v, PARTS) for v in scaled], X_RING)
        with jax.named_scope("back"):

            def blocks(operand, hops):
                return back_blocks(
                    z_up.astype(jnp.int32), x_behind.astype(jnp.int32), operand, space_basis, partner, hops, shards
                )

            back = ring_reduce(blocks, y_lo_pos, Z_UP, Z_DOWN, Y_LO)
            back = [ordered(v[:, :H], v[:, H:], yh, 1) for v in (back[0].astype(BF), back[1].astype(BF))]
            partner_rows = [send(v[128:], CORE) for v in back]
            back = [ordered(v[:128], p, core, 1) for v, p in zip(back, partner_rows)]
        with jax.named_scope("back_gather"):
            pieces += list(gather_both(*back))
    with jax.named_scope("gradient"):
        grad, alpha = gradient(row_at, blk_at, time_row, time_basis, pieces)
    return jnp.transpose(alpha, (2, 0, 1)), grad


def x_other(col_at, x, sign, yh):
    ring = jnp.arange(4, dtype=jnp.int32)
    x_behind = (x + sign * ring) % 4
    return jnp.stack([yh * 8 + x_behind * 2, (1 - yh) * 8 + x_behind * 2], axis=1).reshape(8)


def solution(mesh):
    return jax.shard_map(
        per_device,
        mesh=mesh,
        in_specs=(P("space", None, "tm"), P("space", "tm"), P("tm", None), P(), P()),
        out_specs=(P("space", None, "tm"), P("space", None, "tm")),
        check_vma=False,
    )
```

```python
import functools

import jax
import jax.numpy as jnp
from jax import lax
from jax.experimental import pallas as pl
from jax.experimental.pallas import tpu as pltpu
from jax.sharding import PartitionSpec as P

TIMES = 512
REPS = 2
CHUNKS = 1
U = TIMES // CHUNKS
H = U // 2
PARTS = 2
BF = jnp.bfloat16
F32 = jnp.float32
NT = (((1,), (1,)), ((), ()))
AXES = ("space", "tm")


def vmem():
    return pl.BlockSpec(memory_space=pltpu.VMEM)


def params(mib):
    return pltpu.CompilerParams(vmem_limit_bytes=mib * 1024 * 1024)


def cost(flops, nbytes):
    return pl.CostEstimate(flops=flops, bytes_accessed=nbytes, transcendentals=0)


def route(move):
    pairs = []
    for i in range(128):
        s, t = i // 8, i % 8
        yh, x, c, z, yl = move(s // 8, (s // 2) % 4, s % 2, t // 2, t % 2)
        pairs.append((i, (yh * 8 + (x % 4) * 2 + c) * 8 + (z % 4) * 2 + yl))
    return pairs


X_RING = route(lambda yh, x, c, z, yl: (yh, x + 1 - 2 * c, c, z, yl))
Z_RING = route(lambda yh, x, c, z, yl: (yh, x, c, z + 1 - 2 * c, yl))
X_UP = route(lambda yh, x, c, z, yl: (yh, x + 1, c, z, yl))
X_DOWN = route(lambda yh, x, c, z, yl: (yh, x - 1, c, z, yl))
Z_UP = route(lambda yh, x, c, z, yl: (yh, x, c, z + 1, yl))
Z_DOWN = route(lambda yh, x, c, z, yl: (yh, x, c, z - 1, yl))
Y_HI = route(lambda yh, x, c, z, yl: (1 - yh, x, c, z, yl))
Y_LO = route(lambda yh, x, c, z, yl: (yh, x, c, z, 1 - yl))
CORE = route(lambda yh, x, c, z, yl: (yh, x, 1 - c, z, yl))


def send(v, pairs):
    return lax.ppermute(v, AXES, pairs)


def split(v, parts):
    rows = v.shape[0] // parts
    return [v[rows * i : rows * (i + 1)] for i in range(parts)]


def gather(piece, swap, ring, parts, late=0):
    own = split(piece, parts)
    rounds = parts - late
    other = [send(v, swap) for v in own[:rounds]] if late else split(send(piece, swap), parts)
    hops = []
    for hop in range(4):
        if hop:
            own = [send(v, ring) for v in own]
            other = [send(v, ring) for v in other]
        hops += [own, other + [send(v, swap) for v in own[rounds:]]]
    return hops


def after(v, *others):
    return lax.optimization_barrier((v, *others))[0]


def ring_gather(pieces, ring):
    hops = list(pieces)
    for _ in range(3):
        pieces = [[send(v, ring) for v in parts] for parts in pieces]
        hops += pieces
    return hops


def gather_both(own, other):
    z = [jnp.concatenate([own, other], axis=0)]
    across = send(own, Y_HI)
    first = send(own, X_RING)
    z.append(send(z[0], Z_RING))
    x = [own, jnp.concatenate([across, first], axis=0)]
    x.append(send(after(x[1], z[1]), X_RING))
    z.append(send(z[1], Z_RING))
    x.append(send(after(x[2], z[2]), X_RING))
    z.append(send(z[2], Z_RING))
    x.append(send(after(x[3][:128], z[3]), X_RING))
    return z, x


def ring_reduce(blocks, operand, up, down, swap):
    far = blocks(operand, (2,))
    far, operand = lax.optimization_barrier((far, operand))
    near = blocks(operand, (1, 3))
    got = []
    for half in (1, 0):
        top, bot = split(far[half][0], 2)
        below, above = send(top, up), send(bot, down)
        to_up, to_down = split(near[half][0], 2), split(near[half][1], 2)
        to_up = [(to_up[0] + below.astype(F32)).astype(BF), to_up[1].astype(BF)]
        to_down = [to_down[0].astype(BF), (to_down[1] + above.astype(F32)).astype(BF)]
        to_up, to_down = jnp.concatenate(to_up, axis=0), jnp.concatenate(to_down, axis=0)
        if half:
            to_up, to_down, operand = lax.optimization_barrier((to_up, to_down, operand))
        got.append((send(to_up, up), send(to_down, down)))
    own = blocks(operand, (0,))
    away, kept = [own[h][0] + u.astype(F32) + d.astype(F32) for h, (u, d) in zip((1, 0), got)]
    to_kept, to_away = lax.optimization_barrier((send(away.astype(BF), swap), send(kept.astype(BF), swap)))
    return kept + to_kept.astype(F32), away + to_away.astype(F32)


def hop_at(hops, step):
    return jnp.where(step == 0, hops[0], hops[-1])


def rotate(pos, pieces):
    def kernel(pos_ref, *refs):
        ins, (out_ref, tb_ref, ser_ref) = refs[:-3], refs[-3:]
        for k in range(8):
            for p in range(2):
                ref = ins[2 * k + p]
                at = 64 * k + 32 * p
                tb_ref[at : at + 16] = ref[64:80, :512]
                tb_ref[at + 16 : at + 32] = ref[64:80, 512:]
                ser_ref[64 * k : 64 * (k + 1), 1024 * p : 1024 * (p + 1)] = ref[:64, :]
        tb = tb_ref[...].T
        yh = pos_ref[0]
        for p in range(2):
            cols = slice(1024 * p, 1024 * (p + 1))
            part = jnp.dot(tb, ser_ref[:, cols], preferred_element_type=F32).astype(BF)
            for j in range(2 * CHUNKS):
                half = jnp.where(yh == 0, j % 2, 1 - j % 2)
                row = pl.multiple_of((j // 2) * U + half * H, H)
                out_ref[pl.ds(row, H), cols] = part[j * H : (j + 1) * H]

    return pl.pallas_call(
        kernel,
        out_shape=jax.ShapeDtypeStruct((TIMES, 2048), BF),
        in_specs=[pl.BlockSpec(memory_space=pltpu.SMEM)] + [vmem()] * 16,
        out_specs=vmem(),
        scratch_shapes=[pltpu.VMEM((TIMES, TIMES), BF), pltpu.VMEM((TIMES, 2048), BF)],
        compiler_params=params(48),
        cost_estimate=cost(2 * 512 * 512 * 2048, 6 << 20),
        name="rotate",
    )(pos, *pieces)


def spectral_blocks(idx, chunk, xt, own, partner, hops):
    far = hops[0] == 2
    dtype = BF if far else F32

    def kernel(idx_ref, x_ref, a_ref, b_ref, mine_ref, theirs_ref):
        y = jnp.dot(x_ref[:, :1024], a_ref[...], preferred_element_type=F32)
        y += jnp.dot(x_ref[:, 1024:], b_ref[...], preferred_element_type=F32)
        mine_ref[0] = y[:H].astype(dtype)
        theirs_ref[0] = y[H:].astype(dtype)

    n = len(hops)
    return pl.pallas_call(
        kernel,
        out_shape=[jax.ShapeDtypeStruct((n, H, 512), dtype)] * 2,
        grid_spec=pltpu.PrefetchScalarGridSpec(
            num_scalar_prefetch=1,
            grid=(n,),
            in_specs=[
                pl.BlockSpec((U, 2048), lambda m, i: (chunk, 0)),
                pl.BlockSpec((1024, 512), lambda m, i: (0, i[hop_at(hops, m)])),
                pl.BlockSpec((1024, 512), lambda m, i: (0, i[hop_at(hops, m)])),
            ],
            out_specs=[pl.BlockSpec((1, H, 512), lambda m, i: (m, 0, 0))] * 2,
        ),
        compiler_params=params(48),
        cost_estimate=cost(2 * U * 2048 * 512 * n, (3 << 20) * n),
        name="spectral_far" if far else "spectral_near",
    )(idx, xt, own, partner)


def back_blocks(row_idx, col_idx, pos, own, partner, hops, shards):
    far = hops[0] == 2
    dtype = BF if far else F32
    flat = [v for parts in shards for v in parts]
    rows = flat[0].shape[0]

    def kernel(row_ref, col_ref, pos_ref, a_ref, b_ref, *refs):
        ins, (mine_ref, theirs_ref, s_ref, y_ref) = refs[:-4], refs[-4:]

        @pl.when(pl.program_id(0) == 0)
        def _():
            for k in range(4):
                cols = pl.ds(pl.multiple_of(col_ref[k] * 512, 512), 512)
                per_hop = len(ins) // 4
                for n in range(per_hop):
                    s_ref[rows * n : rows * (n + 1), cols] = ins[per_hop * k + n][...]

        y_ref[:256] = lax.dot_general(a_ref[...], s_ref[...], NT, preferred_element_type=F32)
        y_ref[256:] = lax.dot_general(b_ref[...], s_ref[...], NT, preferred_element_type=F32)
        at = pl.multiple_of(pos_ref[0] * 128, 128)
        off = pl.multiple_of(128 - at, 128)
        mine_ref[0, :128] = y_ref[pl.ds(at, 128)].astype(dtype)
        mine_ref[0, 128:] = y_ref[pl.ds(256 + at, 128)].astype(dtype)
        theirs_ref[0, :128] = y_ref[pl.ds(off, 128)].astype(dtype)
        theirs_ref[0, 128:] = y_ref[pl.ds(256 + off, 128)].astype(dtype)

    n = len(hops)
    return pl.pallas_call(
        kernel,
        out_shape=[jax.ShapeDtypeStruct((n, 256, U), dtype)] * 2,
        grid_spec=pltpu.PrefetchScalarGridSpec(
            num_scalar_prefetch=3,
            grid=(n,),
            in_specs=[pl.BlockSpec((256, 2048), lambda m, r, c, p: (r[hop_at(hops, m)], 0))] * 2
            + [pl.BlockSpec(v.shape, lambda m, r, c, p: (0, 0)) for v in flat],
            out_specs=[pl.BlockSpec((1, 256, U), lambda m, r, c, p: (m, 0, 0))] * 2,
            scratch_shapes=[pltpu.VMEM((U, 2048), BF), pltpu.VMEM((512, U), F32)],
        ),
        compiler_params=params(48),
        cost_estimate=cost(2 * U * 2048 * 512 * n, (3 << 20) * n),
        name="back_far" if far else "back_near",
    )(row_idx, col_idx, pos, own, partner, *flat)


def gradient_half(row_idx, blk_idx, half, time_row, time_basis, rows, cols, grad=None):
    first = grad is None
    arrays = list(rows) + [v for v, _ in cols]
    starts = [(n, r) for n in range(4) for r in (0, 128)] + [(4 + n, r) for n, (_, r) in enumerate(cols)]

    def kernel(row_ref, blk_ref, half_ref, te_ref, tb_ref, *refs):
        ins = refs[:12]
        grad_ref, (r_scr, c_scr, sems) = refs[12 if first else 13], refs[-3:]
        step = pl.program_id(0)

        @pl.when(step == 0)
        def _():
            copies = []
            for n, (array, row) in enumerate(starts):
                scr, at = (r_scr, row_ref[n]) if n < 8 else (c_scr, blk_ref[n - 8])
                place = scr.at[pl.ds(pl.multiple_of(at * 128, 128), 128)]
                copies.append(pltpu.make_async_copy(ins[array].at[row : row + 128], place, sems.at[n]))
            for copy in copies:
                copy.start()
            for copy in copies:
                copy.wait()

        b = r_scr[pl.ds(pl.multiple_of(step * 256, 256), 256), :]
        w = (b.astype(F32) * te_ref[...] / (REPS * TIMES)).astype(BF)
        g = lax.dot_general(w, c_scr[...], NT, preferred_element_type=F32)
        grad_ref[...] = g.astype(BF).reshape(256, 8, 128)
        if first:
            for q in range(REPS):
                lanes = slice(TIMES * q, TIMES * (q + 1))
                al = lax.dot_general(tb_ref[...], b[:, lanes], NT, preferred_element_type=F32)
                refs[13][q] = al.astype(BF)

    out_shape = [jax.ShapeDtypeStruct((1024, 16, 128), BF)]
    out_specs = [pl.BlockSpec((256, 8, 128), lambda m, r, c, h: (m, h[0], 0))]
    if first:
        out_shape.append(jax.ShapeDtypeStruct((REPS, 64, 1024), BF))
        out_specs.append(pl.BlockSpec((REPS, 64, 256), lambda m, r, c, h: (0, 0, m)))
    else:
        arrays.append(grad)
    return pl.pallas_call(
        kernel,
        out_shape=out_shape,
        grid_spec=pltpu.PrefetchScalarGridSpec(
            num_scalar_prefetch=3,
            grid=(4,),
            in_specs=[
                pl.BlockSpec((1, REPS * TIMES), lambda m, r, c, h: (0, 0)),
                pl.BlockSpec((64, TIMES), lambda m, r, c, h: (0, 0)),
            ]
            + [pl.BlockSpec(memory_space=pl.ANY)] * len(arrays),
            out_specs=out_specs,
            scratch_shapes=[
                pltpu.VMEM((1024, REPS * TIMES), BF),
                pltpu.VMEM((1024, REPS * TIMES), BF),
                pltpu.SemaphoreType.DMA((16,)),
            ],
        ),
        input_output_aliases={} if first else {4 + len(arrays): 0},
        compiler_params=params(20),
        cost_estimate=cost(2 * 1024 * 1024 * 1024, 10 << 20),
        name="gradient_own" if first else "gradient_other",
    )(row_idx, blk_idx, half, time_row, time_basis, *arrays)


def ordered(own, other, position, axis):
    first = jnp.where(position == 0, own, other)
    second = jnp.where(position == 0, other, own)
    return jnp.concatenate([first, second], axis=axis)


def per_device(series, space_basis, time_basis, space_eig, time_eig):
    space, tm = lax.axis_index("space"), lax.axis_index("tm")
    yh, x, core = space // 8, (space // 2) % 4, space % 2
    z, yl = tm // 2, tm % 2
    sign = 1 - 2 * core
    ring = jnp.arange(4, dtype=jnp.int32)
    x_up, z_up = (x + ring) % 4, (z + ring) % 4
    x_behind, z_behind = (x - sign * ring) % 4, (z - sign * ring) % 4
    y_lo_pos = jnp.stack([yl]).astype(jnp.int32)
    y_hi_pos = jnp.stack([yh]).astype(jnp.int32)
    row_at = jnp.stack([z_behind * 2 + yl, z_behind * 2 + 1 - yl], axis=1).reshape(8).astype(jnp.int32)
    blk_at = jnp.concatenate([x_behind * 2 + core, (x + sign * ring) % 4 * 2 + 1 - core]).astype(jnp.int32)
    eig_own = lax.dynamic_slice_in_dim(space_eig, tm * 2048 + x * 512, 512)
    time_row = jnp.concatenate(
        [time_eig[U * k : U * (k + 1)] for k in range(CHUNKS) for _ in range(REPS)]
    )[None, :]

    with jax.named_scope("series_gather"):
        turned = jnp.transpose(series, (1, 2, 0))
        mine = lax.dynamic_index_in_dim(turned, core, 0, keepdims=False)
        theirs = lax.dynamic_index_in_dim(turned, 1 - core, 0, keepdims=False)
        theirs = send(theirs, CORE)
        theirs, basis = lax.optimization_barrier((theirs, space_basis))
        partner = send(basis, CORE)
        packs = [jnp.concatenate([time_basis[32 * p : 32 * p + 16], time_basis[32 * p + 16 : 32 * p + 32]], axis=1) for p in range(2)]
        shard = jnp.concatenate([mine, packs[0], theirs, packs[1]], axis=0)
        pieces = [v for parts in gather(shard, Y_LO, Z_RING, 2, late=1) for v in parts]
    with jax.named_scope("rotation"):
        xt = rotate(y_hi_pos, pieces)

    for k in range(CHUNKS):
        with jax.named_scope("spectral"):

            def blocks(operand, hops):
                return spectral_blocks(x_up.astype(jnp.int32), k, operand, space_basis, partner, hops)

            spectral = ring_reduce(blocks, xt, X_UP, X_DOWN, Y_HI)
            scaled = []
            for v, half in zip(spectral, (yh, 1 - yh)):
                eig_rows = lax.dynamic_slice_in_dim(time_eig, k * U + half * H, H)
                denom = eig_rows[:, None] * eig_own[None, :] + 0.1
                scaled.append((v / denom).astype(BF))
        with jax.named_scope("scaled_gather"):
            shards = ring_gather([split(v, PARTS) for v in scaled], X_RING)
        with jax.named_scope("back"):

            def blocks(operand, hops):
                return back_blocks(
                    z_up.astype(jnp.int32), x_behind.astype(jnp.int32), operand, space_basis, partner, hops, shards
                )

            back = ring_reduce(blocks, y_lo_pos, Z_UP, Z_DOWN, Y_LO)
            back = [ordered(v[:, :H], v[:, H:], yh, 1) for v in (back[0].astype(BF), back[1].astype(BF))]
            partner_rows = [send(v[128:], CORE) for v in back]
            back = [ordered(v[:128], p, core, 1) for v, p in zip(back, partner_rows)]
        with jax.named_scope("back_gather"):
            rows, near = gather_both(*back)
            swapped = [send(v, CORE) for v in near[:4]]
    with jax.named_scope("gradient"):
        args = (time_row, time_basis, rows)
        cols = [(v[n], 128 if n else 0) for v in (near, swapped) for n in range(4)]
        grad, alpha = gradient_half(row_at, blk_at, y_hi_pos, *args, cols)
        swapped.append(send(after(near[4], alpha), CORE))
        cols = [(v[n], 0) for v in (near, swapped) for n in range(1, 5)]
        (grad,) = gradient_half(row_at, blk_at, 1 - y_hi_pos, *args, cols, grad)
    return jnp.transpose(alpha, (2, 0, 1)), grad


def solution(mesh):
    return jax.shard_map(
        per_device,
        mesh=mesh,
        in_specs=(P("space", None, "tm"), P("space", "tm"), P("tm", None), P(), P()),
        out_specs=(P("space", None, "tm"), P("space", None, "tm")),
        check_vma=False,
    )
```

```python
import functools

import jax
import jax.numpy as jnp
from jax import lax
from jax.experimental import pallas as pl
from jax.experimental.pallas import tpu as pltpu
from jax.sharding import PartitionSpec as P

TIMES = 512
REPS = 2
CHUNKS = 1
U = TIMES // CHUNKS
H = U // 2
PARTS = 2
BF = jnp.bfloat16
F32 = jnp.float32
NT = (((1,), (1,)), ((), ()))
AXES = ("space", "tm")


def vmem():
    return pl.BlockSpec(memory_space=pltpu.VMEM)


def params(mib):
    return pltpu.CompilerParams(vmem_limit_bytes=mib * 1024 * 1024)


def cost(flops, nbytes):
    return pl.CostEstimate(flops=flops, bytes_accessed=nbytes, transcendentals=0)


def route(move):
    pairs = []
    for i in range(128):
        s, t = i // 8, i % 8
        yh, x, c, z, yl = move(s // 8, (s // 2) % 4, s % 2, t // 2, t % 2)
        pairs.append((i, (yh * 8 + (x % 4) * 2 + c) * 8 + (z % 4) * 2 + yl))
    return pairs


X_RING = route(lambda yh, x, c, z, yl: (yh, x + 1 - 2 * c, c, z, yl))
Z_RING = route(lambda yh, x, c, z, yl: (yh, x, c, z + 1 - 2 * c, yl))
X_UP = route(lambda yh, x, c, z, yl: (yh, x + 1, c, z, yl))
X_DOWN = route(lambda yh, x, c, z, yl: (yh, x - 1, c, z, yl))
Z_UP = route(lambda yh, x, c, z, yl: (yh, x, c, z + 1, yl))
Z_DOWN = route(lambda yh, x, c, z, yl: (yh, x, c, z - 1, yl))
Y_HI = route(lambda yh, x, c, z, yl: (1 - yh, x, c, z, yl))
Y_LO = route(lambda yh, x, c, z, yl: (yh, x, c, z, 1 - yl))
CORE = route(lambda yh, x, c, z, yl: (yh, x, 1 - c, z, yl))


def send(v, pairs):
    return lax.ppermute(v, AXES, pairs)


def split(v, parts):
    rows = v.shape[0] // parts
    return [v[rows * i : rows * (i + 1)] for i in range(parts)]


def gather(own, swap, ring, late):
    rounds = len(own) - late
    other = [send(v, swap) for v in own[:rounds]]
    hops = []
    for hop in range(4):
        if hop:
            own = [send(v, ring) for v in own]
            other = [send(v, ring) for v in other]
        hops += [own, other + [send(v, swap) for v in own[rounds:]]]
    return hops


def after(v, *others):
    return lax.optimization_barrier((v, *others))[0]


def ring_gather(pieces, ring):
    hops = list(pieces)
    for _ in range(3):
        pieces = [[send(v, ring) for v in parts] for parts in pieces]
        hops += pieces
    return hops


def gather_both(own, other):
    z = [jnp.concatenate([own, other], axis=0)]
    across = send(own, Y_HI)
    first = send(own, X_RING)
    z.append(send(z[0], Z_RING))
    x = [own, jnp.concatenate([across, first], axis=0)]
    x.append(send(after(x[1], z[1]), X_RING))
    z.append(send(z[1], Z_RING))
    x.append(send(after(x[2], z[2]), X_RING))
    z.append(send(z[2], Z_RING))
    x.append(send(after(x[3][:128], z[3]), X_RING))
    return z, x


def ring_reduce(blocks, operand, up, down, swap):
    far = blocks(operand, (2,))
    far, operand = lax.optimization_barrier((far, operand))
    near = blocks(operand, (1, 3))
    got = []
    for half in (1, 0):
        top, bot = split(far[half][0], 2)
        below, above = send(top, up), send(bot, down)
        to_up, to_down = split(near[half][0], 2), split(near[half][1], 2)
        to_up = [(to_up[0] + below.astype(F32)).astype(BF), to_up[1].astype(BF)]
        to_down = [to_down[0].astype(BF), (to_down[1] + above.astype(F32)).astype(BF)]
        to_up, to_down = jnp.concatenate(to_up, axis=0), jnp.concatenate(to_down, axis=0)
        if half:
            to_up, to_down, operand = lax.optimization_barrier((to_up, to_down, operand))
        got.append((send(to_up, up), send(to_down, down)))
    own = blocks(operand, (0,))
    away, kept = [own[h][0] + u.astype(F32) + d.astype(F32) for h, (u, d) in zip((1, 0), got)]
    to_kept, to_away = lax.optimization_barrier((send(away.astype(BF), swap), send(kept.astype(BF), swap)))
    return kept + to_kept.astype(F32), away + to_away.astype(F32)


def hop_at(hops, step):
    return jnp.where(step == 0, hops[0], hops[-1])


def rotate(pos, pieces):
    def kernel(pos_ref, *refs):
        ins, (out_ref, tb_ref, ser_ref) = refs[:-3], refs[-3:]
        for k in range(8):
            for p in range(2):
                ref = ins[2 * k + p]
                at = 64 * k + 32 * p
                tb_ref[at : at + 16] = ref[64:80, :512]
                tb_ref[at + 16 : at + 32] = ref[64:80, 512:]
                ser_ref[64 * k : 64 * (k + 1), 1024 * p : 1024 * (p + 1)] = ref[:64, :]
        tb = tb_ref[...].T
        yh = pos_ref[0]
        for p in range(2):
            cols = slice(1024 * p, 1024 * (p + 1))
            part = jnp.dot(tb, ser_ref[:, cols], preferred_element_type=F32).astype(BF)
            for j in range(2 * CHUNKS):
                half = jnp.where(yh == 0, j % 2, 1 - j % 2)
                row = pl.multiple_of((j // 2) * U + half * H, H)
                out_ref[pl.ds(row, H), cols] = part[j * H : (j + 1) * H]

    return pl.pallas_call(
        kernel,
        out_shape=jax.ShapeDtypeStruct((TIMES, 2048), BF),
        in_specs=[pl.BlockSpec(memory_space=pltpu.SMEM)] + [vmem()] * 16,
        out_specs=vmem(),
        scratch_shapes=[pltpu.VMEM((TIMES, TIMES), BF), pltpu.VMEM((TIMES, 2048), BF)],
        compiler_params=params(48),
        cost_estimate=cost(2 * 512 * 512 * 2048, 6 << 20),
        name="rotate",
    )(pos, *pieces)


def spectral_blocks(idx, chunk, xt, own, partner, hops):
    far = hops[0] == 2
    dtype = BF if far else F32

    def kernel(idx_ref, x_ref, a_ref, b_ref, mine_ref, theirs_ref):
        y = jnp.dot(x_ref[:, :1024], a_ref[...], preferred_element_type=F32)
        y += jnp.dot(x_ref[:, 1024:], b_ref[...], preferred_element_type=F32)
        mine_ref[0] = y[:H].astype(dtype)
        theirs_ref[0] = y[H:].astype(dtype)

    n = len(hops)
    return pl.pallas_call(
        kernel,
        out_shape=[jax.ShapeDtypeStruct((n, H, 512), dtype)] * 2,
        grid_spec=pltpu.PrefetchScalarGridSpec(
            num_scalar_prefetch=1,
            grid=(n,),
            in_specs=[
                pl.BlockSpec((U, 2048), lambda m, i: (chunk, 0)),
                pl.BlockSpec((1024, 512), lambda m, i: (0, i[hop_at(hops, m)])),
                pl.BlockSpec((1024, 512), lambda m, i: (0, i[hop_at(hops, m)])),
            ],
            out_specs=[pl.BlockSpec((1, H, 512), lambda m, i: (m, 0, 0))] * 2,
        ),
        compiler_params=params(48),
        cost_estimate=cost(2 * U * 2048 * 512 * n, (3 << 20) * n),
        name="spectral_far" if far else "spectral_near",
    )(idx, xt, own, partner)


def back_early(col_idx, own, partner, pieces):
    hops = len(pieces) // 4
    rows = pieces[0].shape[0]

    def kernel(col_ref, a_ref, b_ref, *refs):
        ins, (acc_ref, s_ref) = refs[:-2], refs[-2:]

        @pl.when(pl.program_id(0) == 0)
        def _():
            for n, ref in enumerate(ins):
                s_ref[n // 4, rows * (n % 4) : rows * (n % 4 + 1)] = ref[...]

        for c, block in enumerate((a_ref, b_ref)):
            total = jnp.zeros((256, U), F32)
            for k in range(hops):
                cols = pl.ds(pl.multiple_of(col_ref[k] * 512, 512), 512)
                total += lax.dot_general(block[:, cols], s_ref[k], NT, preferred_element_type=F32)
            acc_ref[c] = total

    return pl.pallas_call(
        kernel,
        out_shape=jax.ShapeDtypeStruct((2, 1024, U), F32),
        grid_spec=pltpu.PrefetchScalarGridSpec(
            num_scalar_prefetch=1,
            grid=(4,),
            in_specs=[pl.BlockSpec((256, 2048), lambda m, c: (m, 0))] * 2
            + [pl.BlockSpec(v.shape, lambda m, c: (0, 0)) for v in pieces],
            out_specs=pl.BlockSpec((2, 256, U), lambda m, c: (0, m, 0)),
            scratch_shapes=[pltpu.VMEM((hops, U, 512), BF)],
        ),
        compiler_params=params(48),
        cost_estimate=cost(2 * U * 2048 * 512 * hops, 10 << 20),
        name="back_early",
    )(col_idx, own, partner, *pieces)


def back_blocks(row_idx, col_idx, pos, own, partner, pieces, early, blocks):
    far = blocks[0] == 2
    dtype = BF if far else F32
    rows = pieces[0].shape[0]
    half = len(pieces) // 2

    def kernel(row_ref, col_ref, pos_ref, a2_ref, a3_ref, b2_ref, b3_ref, acc_ref, *refs):
        ins, (mine_ref, theirs_ref, s_ref, y_ref) = refs[:-4], refs[-4:]

        @pl.when(pl.program_id(0) == 0)
        def _():
            for n, ref in enumerate(ins):
                s_ref[n // half, rows * (n % half) : rows * (n % half + 1)] = ref[...]

        for c, pair in enumerate(((a2_ref, a3_ref), (b2_ref, b3_ref))):
            total = acc_ref[c]
            for k in range(2):
                total += lax.dot_general(pair[k][...], s_ref[k], NT, preferred_element_type=F32)
            y_ref[256 * c : 256 * (c + 1)] = total
        at = pl.multiple_of(pos_ref[0] * 128, 128)
        off = pl.multiple_of(128 - at, 128)
        for c in range(2):
            mine_ref[0, 128 * c : 128 * (c + 1)] = y_ref[pl.ds(256 * c + at, 128)].astype(dtype)
            theirs_ref[0, 128 * c : 128 * (c + 1)] = y_ref[pl.ds(256 * c + off, 128)].astype(dtype)

    n = len(blocks)

    def a_spec(hop):
        return pl.BlockSpec((256, 512), lambda m, r, c, p: (r[hop_at(blocks, m)], c[hop]))

    return pl.pallas_call(
        kernel,
        out_shape=[jax.ShapeDtypeStruct((n, 256, U), dtype)] * 2,
        grid_spec=pltpu.PrefetchScalarGridSpec(
            num_scalar_prefetch=3,
            grid=(n,),
            in_specs=[a_spec(2), a_spec(3)] * 2
            + [pl.BlockSpec((2, 256, U), lambda m, r, c, p: (0, r[hop_at(blocks, m)], 0))]
            + [pl.BlockSpec(v.shape, lambda m, r, c, p: (0, 0)) for v in pieces],
            out_specs=[pl.BlockSpec((1, 256, U), lambda m, r, c, p: (m, 0, 0))] * 2,
            scratch_shapes=[pltpu.VMEM((2, U, 512), BF), pltpu.VMEM((512, U), F32)],
        ),
        compiler_params=params(48),
        cost_estimate=cost(2 * U * 1024 * 512 * n, (3 << 20) * n),
        name="back_far" if far else "back_near",
    )(row_idx, col_idx, pos, own, own, partner, partner, early, *pieces)


def gradient_half(row_idx, blk_idx, half, time_row, time_basis, rows, cols, grad=None):
    first = grad is None
    arrays = list(rows) + [v for v, _ in cols]
    starts = [(n, r) for n in range(4) for r in (0, 128)] + [(4 + n, r) for n, (_, r) in enumerate(cols)]

    def kernel(row_ref, blk_ref, half_ref, te_ref, tb_ref, *refs):
        ins = refs[:12]
        grad_ref, (r_scr, c_scr, sems) = refs[12 if first else 13], refs[-3:]
        step = pl.program_id(0)

        @pl.when(step == 0)
        def _():
            copies = []
            for n, (array, row) in enumerate(starts):
                scr, at = (r_scr, row_ref[n]) if n < 8 else (c_scr, blk_ref[n - 8])
                place = scr.at[pl.ds(pl.multiple_of(at * 128, 128), 128)]
                copies.append(pltpu.make_async_copy(ins[array].at[row : row + 128], place, sems.at[n]))
            for copy in copies:
                copy.start()
            for copy in copies:
                copy.wait()

        b = r_scr[pl.ds(pl.multiple_of(step * 256, 256), 256), :]
        w = (b.astype(F32) * te_ref[...] / (REPS * TIMES)).astype(BF)
        g = lax.dot_general(w, c_scr[...], NT, preferred_element_type=F32)
        grad_ref[...] = g.astype(BF).reshape(256, 8, 128)
        if first:
            for q in range(REPS):
                lanes = slice(TIMES * q, TIMES * (q + 1))
                al = lax.dot_general(tb_ref[...], b[:, lanes], NT, preferred_element_type=F32)
                refs[13][q] = al.astype(BF)

    out_shape = [jax.ShapeDtypeStruct((1024, 16, 128), BF)]
    out_specs = [pl.BlockSpec((256, 8, 128), lambda m, r, c, h: (m, h[0], 0))]
    if first:
        out_shape.append(jax.ShapeDtypeStruct((REPS, 64, 1024), BF))
        out_specs.append(pl.BlockSpec((REPS, 64, 256), lambda m, r, c, h: (0, 0, m)))
    else:
        arrays.append(grad)
    return pl.pallas_call(
        kernel,
        out_shape=out_shape,
        grid_spec=pltpu.PrefetchScalarGridSpec(
            num_scalar_prefetch=3,
            grid=(4,),
            in_specs=[
                pl.BlockSpec((1, REPS * TIMES), lambda m, r, c, h: (0, 0)),
                pl.BlockSpec((64, TIMES), lambda m, r, c, h: (0, 0)),
            ]
            + [pl.BlockSpec(memory_space=pl.ANY)] * len(arrays),
            out_specs=out_specs,
            scratch_shapes=[
                pltpu.VMEM((1024, REPS * TIMES), BF),
                pltpu.VMEM((1024, REPS * TIMES), BF),
                pltpu.SemaphoreType.DMA((16,)),
            ],
        ),
        input_output_aliases={} if first else {4 + len(arrays): 0},
        compiler_params=params(20),
        cost_estimate=cost(2 * 1024 * 1024 * 1024, 10 << 20),
        name="gradient_own" if first else "gradient_other",
    )(row_idx, blk_idx, half, time_row, time_basis, *arrays)


def ordered(own, other, position, axis):
    first = jnp.where(position == 0, own, other)
    second = jnp.where(position == 0, other, own)
    return jnp.concatenate([first, second], axis=axis)


def per_device(series, space_basis, time_basis, space_eig, time_eig):
    space, tm = lax.axis_index("space"), lax.axis_index("tm")
    yh, x, core = space // 8, (space // 2) % 4, space % 2
    z, yl = tm // 2, tm % 2
    sign = 1 - 2 * core
    ring = jnp.arange(4, dtype=jnp.int32)
    x_up, z_up = (x + ring) % 4, (z + ring) % 4
    x_behind, z_behind = (x - sign * ring) % 4, (z - sign * ring) % 4
    y_lo_pos = jnp.stack([yl]).astype(jnp.int32)
    y_hi_pos = jnp.stack([yh]).astype(jnp.int32)
    row_at = jnp.stack([z_behind * 2 + yl, z_behind * 2 + 1 - yl], axis=1).reshape(8).astype(jnp.int32)
    blk_at = jnp.concatenate([x_behind * 2 + core, (x + sign * ring) % 4 * 2 + 1 - core]).astype(jnp.int32)
    eig_own = lax.dynamic_slice_in_dim(space_eig, tm * 2048 + x * 512, 512)
    time_row = jnp.concatenate(
        [time_eig[U * k : U * (k + 1)] for k in range(CHUNKS) for _ in range(REPS)]
    )[None, :]

    with jax.named_scope("series_gather"):
        turned = jnp.transpose(series, (1, 2, 0))
        mine = lax.dynamic_index_in_dim(turned, core, 0, keepdims=False)
        theirs = lax.dynamic_index_in_dim(turned, 1 - core, 0, keepdims=False)
        theirs = send(theirs, CORE)
        packs = [jnp.concatenate([time_basis[32 * p : 32 * p + 16], time_basis[32 * p + 16 : 32 * p + 32]], axis=1) for p in range(2)]
        shard = [jnp.concatenate([mine, packs[0]], axis=0), jnp.concatenate([theirs, packs[1]], axis=0)]
        *shard, basis = lax.optimization_barrier((*shard, space_basis))
        partner = send(basis, CORE)
        pieces = [v for parts in gather(shard, Y_LO, Z_RING, late=1) for v in parts]
    with jax.named_scope("rotation"):
        xt = rotate(y_hi_pos, pieces)

    for k in range(CHUNKS):
        with jax.named_scope("spectral"):

            def blocks(operand, hops):
                return spectral_blocks(x_up.astype(jnp.int32), k, operand, space_basis, partner, hops)

            spectral = ring_reduce(blocks, xt, X_UP, X_DOWN, Y_HI)
            scaled = []
            for v, half in zip(spectral, (yh, 1 - yh)):
                eig_rows = lax.dynamic_slice_in_dim(time_eig, k * U + half * H, H)
                denom = eig_rows[:, None] * eig_own[None, :] + 0.1
                scaled.append((v / denom).astype(BF))
        with jax.named_scope("scaled_gather"):
            shards = ring_gather([split(v, PARTS) for v in scaled], X_RING)
        with jax.named_scope("back"):

            flat = [v for parts in shards for v in parts]
            behind = x_behind.astype(jnp.int32)
            early = back_early(behind, space_basis, partner, flat[:8])

            def blocks(operand, hops):
                return back_blocks(z_up.astype(jnp.int32), behind, operand, space_basis, partner, flat[8:], early, hops)

            back = ring_reduce(blocks, y_lo_pos, Z_UP, Z_DOWN, Y_LO)
            back = [ordered(v[:, :H], v[:, H:], yh, 1) for v in (back[0].astype(BF), back[1].astype(BF))]
            partner_rows = [send(v[128:], CORE) for v in back]
            back = [ordered(v[:128], p, core, 1) for v, p in zip(back, partner_rows)]
        with jax.named_scope("back_gather"):
            rows, near = gather_both(*back)
            swapped = [send(v, CORE) for v in near[:4]]
    with jax.named_scope("gradient"):
        args = (time_row, time_basis, rows)
        cols = [(v[n], 128 if n else 0) for v in (near, swapped) for n in range(4)]
        grad, alpha = gradient_half(row_at, blk_at, y_hi_pos, *args, cols)
        swapped.append(send(after(near[4], alpha), CORE))
        cols = [(v[n], 0) for v in (near, swapped) for n in range(1, 5)]
        (grad,) = gradient_half(row_at, blk_at, 1 - y_hi_pos, *args, cols, grad)
    return jnp.transpose(alpha, (2, 0, 1)), grad


def solution(mesh):
    return jax.shard_map(
        per_device,
        mesh=mesh,
        in_specs=(P("space", None, "tm"), P("space", "tm"), P("tm", None), P(), P()),
        out_specs=(P("space", None, "tm"), P("space", None, "tm")),
        check_vma=False,
    )
```

```python
import functools

import jax
import jax.numpy as jnp
from jax import lax
from jax.experimental import pallas as pl
from jax.experimental.pallas import tpu as pltpu
from jax.sharding import PartitionSpec as P

TIMES = 512
REPS = 2
CHUNKS = 1
U = TIMES // CHUNKS
H = U // 2
PARTS = 2
BF = jnp.bfloat16
F32 = jnp.float32
NT = (((1,), (1,)), ((), ()))
AXES = ("space", "tm")


def vmem():
    return pl.BlockSpec(memory_space=pltpu.VMEM)


def params(mib):
    return pltpu.CompilerParams(vmem_limit_bytes=mib * 1024 * 1024)


def cost(flops, nbytes):
    return pl.CostEstimate(flops=flops, bytes_accessed=nbytes, transcendentals=0)


def route(move):
    pairs = []
    for i in range(128):
        s, t = i // 8, i % 8
        yh, x, c, z, yl = move(s // 8, (s // 2) % 4, s % 2, t // 2, t % 2)
        pairs.append((i, (yh * 8 + (x % 4) * 2 + c) * 8 + (z % 4) * 2 + yl))
    return pairs


X_RING = route(lambda yh, x, c, z, yl: (yh, x + 1 - 2 * c, c, z, yl))
Z_RING = route(lambda yh, x, c, z, yl: (yh, x, c, z + 1 - 2 * c, yl))
X_UP = route(lambda yh, x, c, z, yl: (yh, x + 1, c, z, yl))
X_DOWN = route(lambda yh, x, c, z, yl: (yh, x - 1, c, z, yl))
Z_UP = route(lambda yh, x, c, z, yl: (yh, x, c, z + 1, yl))
Z_DOWN = route(lambda yh, x, c, z, yl: (yh, x, c, z - 1, yl))
Y_HI = route(lambda yh, x, c, z, yl: (1 - yh, x, c, z, yl))
Y_LO = route(lambda yh, x, c, z, yl: (yh, x, c, z, 1 - yl))
CORE = route(lambda yh, x, c, z, yl: (yh, x, 1 - c, z, yl))


def send(v, pairs):
    return lax.ppermute(v, AXES, pairs)


def split(v, parts):
    rows = v.shape[0] // parts
    return [v[rows * i : rows * (i + 1)] for i in range(parts)]


def gather(own, swap, ring, late):
    rounds = len(own) - late
    other = [send(v, swap) for v in own[:rounds]]
    hops = []
    for hop in range(4):
        if hop:
            own = [send(v, ring) for v in own]
            other = [send(v, ring) for v in other]
        hops += [own, other + [send(v, swap) for v in own[rounds:]]]
    return hops


def after(v, *others):
    return lax.optimization_barrier((v, *others))[0]


def ring_gather(pieces, ring):
    hops = list(pieces)
    for _ in range(3):
        pieces = [[send(v, ring) for v in parts] for parts in pieces]
        hops += pieces
    return hops


def gather_both(own, other):
    pair = jnp.concatenate([own, other], axis=0)
    across = send(own, Y_HI)
    x_below, x_above = send(own, X_UP), send(own, X_DOWN)
    z_below, z_above = send(pair, Z_UP), send(pair, Z_DOWN)
    near = jnp.concatenate([z_below, z_above], axis=0)
    to_up = after(jnp.concatenate([across, x_below[:64]], axis=0), near)
    to_down = after(jnp.concatenate([across, x_above[64:]], axis=0), near)
    from_below, from_above = send(to_up, X_UP), send(to_down, X_DOWN)
    z_far, z_far_other = send(z_below[:128], Z_UP), send(z_above[128:], Z_DOWN)
    far = jnp.concatenate([z_far, z_far_other], axis=0)
    last_below = send(after(from_below[:64], far), X_UP)
    last_above = send(after(from_above[64:128], far), X_DOWN)
    rows = [(pair, r, 128, r // 128, 0) for r in (0, 128)]
    rows += [(near, 128 * n, 128, place, 0) for n, place in enumerate((6, 7, 2, 3))]
    rows += [(far, 0, 128, 4, 0), (far, 128, 128, 5, 0)]
    mine = [(own, 0, 128, 0, 0), (x_below, 0, 128, 3, 0), (x_above, 0, 128, 1, 0)]
    mine += [(from_below, 128, 64, 2, 0), (from_above, 128, 64, 2, 64)]
    theirs = [(across, 0, 128, 0, 0), (from_below, 0, 128, 3, 0), (from_above, 0, 128, 1, 0)]
    theirs += [(last_below, 0, 64, 2, 0), (last_above, 0, 64, 2, 64)]
    return rows, mine, theirs


def ring_reduce(blocks, operand, up, down, swap):
    far = blocks(operand, (2,))
    far, operand = lax.optimization_barrier((far, operand))
    near = blocks(operand, (1, 3))
    got = []
    for half in (1, 0):
        top, bot = split(far[half][0], 2)
        below, above = send(top, up), send(bot, down)
        to_up, to_down = split(near[half][0], 2), split(near[half][1], 2)
        to_up = [(to_up[0] + below.astype(F32)).astype(BF), to_up[1].astype(BF)]
        to_down = [to_down[0].astype(BF), (to_down[1] + above.astype(F32)).astype(BF)]
        to_up, to_down = jnp.concatenate(to_up, axis=0), jnp.concatenate(to_down, axis=0)
        if half:
            to_up, to_down, operand = lax.optimization_barrier((to_up, to_down, operand))
        got.append((send(to_up, up), send(to_down, down)))
    own = blocks(operand, (0,))
    away, kept = [own[h][0] + u.astype(F32) + d.astype(F32) for h, (u, d) in zip((1, 0), got)]
    to_kept, to_away = lax.optimization_barrier((send(away.astype(BF), swap), send(kept.astype(BF), swap)))
    return kept + to_kept.astype(F32), away + to_away.astype(F32)


def hop_at(hops, step):
    return jnp.where(step == 0, hops[0], hops[-1])


def rotate(pos, pieces):
    def kernel(pos_ref, *refs):
        ins, (out_ref, tb_ref, ser_ref) = refs[:-3], refs[-3:]
        for k in range(8):
            for p in range(2):
                ref = ins[2 * k + p]
                at = 64 * k + 32 * p
                tb_ref[at : at + 16] = ref[64:80, :512]
                tb_ref[at + 16 : at + 32] = ref[64:80, 512:]
                ser_ref[64 * k : 64 * (k + 1), 1024 * p : 1024 * (p + 1)] = ref[:64, :]
        tb = tb_ref[...].T
        yh = pos_ref[0]
        for p in range(2):
            cols = slice(1024 * p, 1024 * (p + 1))
            part = jnp.dot(tb, ser_ref[:, cols], preferred_element_type=F32).astype(BF)
            for j in range(2 * CHUNKS):
                half = jnp.where(yh == 0, j % 2, 1 - j % 2)
                row = pl.multiple_of((j // 2) * U + half * H, H)
                out_ref[pl.ds(row, H), cols] = part[j * H : (j + 1) * H]

    return pl.pallas_call(
        kernel,
        out_shape=jax.ShapeDtypeStruct((TIMES, 2048), BF),
        in_specs=[pl.BlockSpec(memory_space=pltpu.SMEM)] + [vmem()] * 16,
        out_specs=vmem(),
        scratch_shapes=[pltpu.VMEM((TIMES, TIMES), BF), pltpu.VMEM((TIMES, 2048), BF)],
        compiler_params=params(48),
        cost_estimate=cost(2 * 512 * 512 * 2048, 6 << 20),
        name="rotate",
    )(pos, *pieces)


def spectral_blocks(idx, chunk, xt, own, partner, hops):
    far = hops[0] == 2
    dtype = BF if far else F32

    def kernel(idx_ref, x_ref, a_ref, b_ref, mine_ref, theirs_ref):
        y = jnp.dot(x_ref[:, :1024], a_ref[...], preferred_element_type=F32)
        y += jnp.dot(x_ref[:, 1024:], b_ref[...], preferred_element_type=F32)
        mine_ref[0] = y[:H].astype(dtype)
        theirs_ref[0] = y[H:].astype(dtype)

    n = len(hops)
    return pl.pallas_call(
        kernel,
        out_shape=[jax.ShapeDtypeStruct((n, H, 512), dtype)] * 2,
        grid_spec=pltpu.PrefetchScalarGridSpec(
            num_scalar_prefetch=1,
            grid=(n,),
            in_specs=[
                pl.BlockSpec((U, 2048), lambda m, i: (chunk, 0)),
                pl.BlockSpec((1024, 512), lambda m, i: (0, i[hop_at(hops, m)])),
                pl.BlockSpec((1024, 512), lambda m, i: (0, i[hop_at(hops, m)])),
            ],
            out_specs=[pl.BlockSpec((1, H, 512), lambda m, i: (m, 0, 0))] * 2,
        ),
        compiler_params=params(48),
        cost_estimate=cost(2 * U * 2048 * 512 * n, (3 << 20) * n),
        name="spectral_far" if far else "spectral_near",
    )(idx, xt, own, partner)


def back_early(col_idx, own, partner, pieces):
    hops = len(pieces) // 4
    rows = pieces[0].shape[0]

    def kernel(col_ref, a_ref, b_ref, *refs):
        ins, (acc_ref, s_ref) = refs[:-2], refs[-2:]

        @pl.when(pl.program_id(0) == 0)
        def _():
            for n, ref in enumerate(ins):
                s_ref[n // 4, rows * (n % 4) : rows * (n % 4 + 1)] = ref[...]

        for c, block in enumerate((a_ref, b_ref)):
            total = jnp.zeros((256, U), F32)
            for k in range(hops):
                cols = pl.ds(pl.multiple_of(col_ref[k] * 512, 512), 512)
                total += lax.dot_general(block[:, cols], s_ref[k], NT, preferred_element_type=F32)
            acc_ref[c] = total

    return pl.pallas_call(
        kernel,
        out_shape=jax.ShapeDtypeStruct((2, 1024, U), F32),
        grid_spec=pltpu.PrefetchScalarGridSpec(
            num_scalar_prefetch=1,
            grid=(4,),
            in_specs=[pl.BlockSpec((256, 2048), lambda m, c: (m, 0))] * 2
            + [pl.BlockSpec(v.shape, lambda m, c: (0, 0)) for v in pieces],
            out_specs=pl.BlockSpec((2, 256, U), lambda m, c: (0, m, 0)),
            scratch_shapes=[pltpu.VMEM((hops, U, 512), BF)],
        ),
        compiler_params=params(48),
        cost_estimate=cost(2 * U * 2048 * 512 * hops, 10 << 20),
        name="back_early",
    )(col_idx, own, partner, *pieces)


def back_blocks(row_idx, col_idx, pos, own, partner, pieces, early, blocks):
    far = blocks[0] == 2
    dtype = BF if far else F32
    rows = pieces[0].shape[0]
    half = len(pieces) // 2

    def kernel(row_ref, col_ref, pos_ref, a2_ref, a3_ref, b2_ref, b3_ref, acc_ref, *refs):
        ins, (mine_ref, theirs_ref, s_ref, y_ref) = refs[:-4], refs[-4:]

        @pl.when(pl.program_id(0) == 0)
        def _():
            for n, ref in enumerate(ins):
                s_ref[n // half, rows * (n % half) : rows * (n % half + 1)] = ref[...]

        for c, pair in enumerate(((a2_ref, a3_ref), (b2_ref, b3_ref))):
            total = acc_ref[c]
            for k in range(2):
                total += lax.dot_general(pair[k][...], s_ref[k], NT, preferred_element_type=F32)
            y_ref[256 * c : 256 * (c + 1)] = total
        at = pl.multiple_of(pos_ref[0] * 128, 128)
        off = pl.multiple_of(128 - at, 128)
        for c in range(2):
            mine_ref[0, 128 * c : 128 * (c + 1)] = y_ref[pl.ds(256 * c + at, 128)].astype(dtype)
            theirs_ref[0, 128 * c : 128 * (c + 1)] = y_ref[pl.ds(256 * c + off, 128)].astype(dtype)

    n = len(blocks)

    def a_spec(hop):
        return pl.BlockSpec((256, 512), lambda m, r, c, p: (r[hop_at(blocks, m)], c[hop]))

    return pl.pallas_call(
        kernel,
        out_shape=[jax.ShapeDtypeStruct((n, 256, U), dtype)] * 2,
        grid_spec=pltpu.PrefetchScalarGridSpec(
            num_scalar_prefetch=3,
            grid=(n,),
            in_specs=[a_spec(2), a_spec(3)] * 2
            + [pl.BlockSpec((2, 256, U), lambda m, r, c, p: (0, r[hop_at(blocks, m)], 0))]
            + [pl.BlockSpec(v.shape, lambda m, r, c, p: (0, 0)) for v in pieces],
            out_specs=[pl.BlockSpec((1, 256, U), lambda m, r, c, p: (m, 0, 0))] * 2,
            scratch_shapes=[pltpu.VMEM((2, U, 512), BF), pltpu.VMEM((512, U), F32)],
        ),
        compiler_params=params(48),
        cost_estimate=cost(2 * U * 1024 * 512 * n, (3 << 20) * n),
        name="back_far" if far else "back_near",
    )(row_idx, col_idx, pos, own, own, partner, partner, early, *pieces)


def gradient_half(row_idx, blk_idx, half, time_row, time_basis, rows, cols, grad=None):
    first = grad is None
    moves = (rows if first else []) + cols
    n_rows = len(moves) - len(cols)
    arrays = []
    for v, *_ in moves:
        if not any(v is w for w in arrays):
            arrays.append(v)
    which = [[v is w for w in arrays].index(True) for v, *_ in moves]

    def kernel(row_ref, blk_ref, half_ref, te_ref, tb_ref, w_ref, *refs):
        ins = refs[: len(arrays)]
        outs = refs[len(arrays) + (0 if first else 1) : -3]
        r_scr, c_scr, sems = refs[-3:]
        step = pl.program_id(0)

        @pl.when(step == 0)
        def _():
            copies = []
            for n, (_, row, size, place, offset) in enumerate(moves):
                scr, at = (r_scr, row_ref[place]) if n < n_rows else (c_scr, blk_ref[place])
                start = pl.multiple_of(at * 128 + offset, 64)
                copies.append(
                    pltpu.make_async_copy(ins[which[n]].at[row : row + size], scr.at[pl.ds(start, size)], sems.at[n])
                )
            for copy in copies:
                copy.start()
            for copy in copies:
                copy.wait()

        if first:
            b = r_scr[pl.ds(pl.multiple_of(step * 256, 256), 256), :]
            w = (b.astype(F32) * te_ref[...] / (REPS * TIMES)).astype(BF)
            outs[2][...] = w
            for q in range(REPS):
                lanes = slice(TIMES * q, TIMES * (q + 1))
                al = lax.dot_general(tb_ref[...], b[:, lanes], NT, preferred_element_type=F32)
                outs[1][q] = al.astype(BF)
        else:
            w = w_ref[...]
        g = lax.dot_general(w, c_scr[...], NT, preferred_element_type=F32)
        outs[0][...] = g.astype(BF).reshape(256, 8, 128)

    wide = REPS * TIMES
    out_shape = [jax.ShapeDtypeStruct((1024, 16, 128), BF)]
    out_specs = [pl.BlockSpec((256, 8, 128), lambda m, r, c, h: (m, h[0], 0))]
    weighted = pl.BlockSpec((256, wide), lambda m, r, c, h: (m, 0))
    if first:
        out_shape += [jax.ShapeDtypeStruct((REPS, 64, 1024), BF), jax.ShapeDtypeStruct((1024, wide), BF)]
        out_specs += [pl.BlockSpec((REPS, 64, 256), lambda m, r, c, h: (0, 0, m)), weighted]
    operands = arrays + ([] if first else [grad])
    return pl.pallas_call(
        kernel,
        out_shape=out_shape,
        grid_spec=pltpu.PrefetchScalarGridSpec(
            num_scalar_prefetch=3,
            grid=(4,),
            in_specs=[
                pl.BlockSpec((1, wide), lambda m, r, c, h: (0, 0)),
                pl.BlockSpec((64, TIMES), lambda m, r, c, h: (0, 0)),
                pl.BlockSpec((1, wide), lambda m, r, c, h: (0, 0)) if first else weighted,
            ]
            + [pl.BlockSpec(memory_space=pl.ANY)] * len(operands),
            out_specs=out_specs,
            scratch_shapes=[
                pltpu.VMEM((1024 if first else 8, wide), BF),
                pltpu.VMEM((1024, wide), BF),
                pltpu.SemaphoreType.DMA((len(moves),)),
            ],
        ),
        input_output_aliases={} if first else {5 + len(operands): 0},
        compiler_params=params(20),
        cost_estimate=cost(2 * 1024 * 1024 * 1024, 10 << 20),
        name="gradient_own" if first else "gradient_other",
    )(row_idx, blk_idx, half, time_row, time_basis, time_row if first else rows, *operands)


def both_cores(pieces, done):
    swapped = []
    for v, *where in pieces:
        if id(v) not in done:
            done[id(v)] = send(v, CORE)
        swapped.append((done[id(v)], where[0], where[1], where[2] + 4, where[3]))
    return pieces + swapped


def ordered(own, other, position, axis):
    first = jnp.where(position == 0, own, other)
    second = jnp.where(position == 0, other, own)
    return jnp.concatenate([first, second], axis=axis)


def per_device(series, space_basis, time_basis, space_eig, time_eig):
    space, tm = lax.axis_index("space"), lax.axis_index("tm")
    yh, x, core = space // 8, (space // 2) % 4, space % 2
    z, yl = tm // 2, tm % 2
    sign = 1 - 2 * core
    ring = jnp.arange(4, dtype=jnp.int32)
    x_up, z_up = (x + ring) % 4, (z + ring) % 4
    x_behind, z_behind = (x - sign * ring) % 4, (z - sign * ring) % 4
    y_lo_pos = jnp.stack([yl]).astype(jnp.int32)
    y_hi_pos = jnp.stack([yh]).astype(jnp.int32)
    row_at = jnp.stack([z_up * 2 + yl, z_up * 2 + 1 - yl], axis=1).reshape(8).astype(jnp.int32)
    blk_at = jnp.concatenate([x_up * 2 + core, x_up * 2 + 1 - core]).astype(jnp.int32)
    eig_own = lax.dynamic_slice_in_dim(space_eig, tm * 2048 + x * 512, 512)
    time_row = jnp.concatenate(
        [time_eig[U * k : U * (k + 1)] for k in range(CHUNKS) for _ in range(REPS)]
    )[None, :]

    with jax.named_scope("series_gather"):
        turned = jnp.transpose(series, (1, 2, 0))
        mine = lax.dynamic_index_in_dim(turned, core, 0, keepdims=False)
        theirs = lax.dynamic_index_in_dim(turned, 1 - core, 0, keepdims=False)
        theirs = send(theirs, CORE)
        packs = [jnp.concatenate([time_basis[32 * p : 32 * p + 16], time_basis[32 * p + 16 : 32 * p + 32]], axis=1) for p in range(2)]
        shard = [jnp.concatenate([mine, packs[0]], axis=0), jnp.concatenate([theirs, packs[1]], axis=0)]
        *shard, basis = lax.optimization_barrier((*shard, space_basis))
        partner = send(basis, CORE)
        pieces = [v for parts in gather(shard, Y_LO, Z_RING, late=1) for v in parts]
    with jax.named_scope("rotation"):
        xt = rotate(y_hi_pos, pieces)

    for k in range(CHUNKS):
        with jax.named_scope("spectral"):

            def blocks(operand, hops):
                return spectral_blocks(x_up.astype(jnp.int32), k, operand, space_basis, partner, hops)

            spectral = ring_reduce(blocks, xt, X_UP, X_DOWN, Y_HI)
            scaled = []
            for v, half in zip(spectral, (yh, 1 - yh)):
                eig_rows = lax.dynamic_slice_in_dim(time_eig, k * U + half * H, H)
                denom = eig_rows[:, None] * eig_own[None, :] + 0.1
                scaled.append((v / denom).astype(BF))
        with jax.named_scope("scaled_gather"):
            shards = ring_gather([split(v, PARTS) for v in scaled], X_RING)
        with jax.named_scope("back"):

            flat = [v for parts in shards for v in parts]
            behind = x_behind.astype(jnp.int32)
            early = back_early(behind, space_basis, partner, flat[:8])

            def blocks(operand, hops):
                return back_blocks(z_up.astype(jnp.int32), behind, operand, space_basis, partner, flat[8:], early, hops)

            back = ring_reduce(blocks, y_lo_pos, Z_UP, Z_DOWN, Y_LO)
            back = [ordered(v[:, :H], v[:, H:], yh, 1) for v in (back[0].astype(BF), back[1].astype(BF))]
            partner_rows = [send(v[128:], CORE) for v in back]
            back = [ordered(v[:128], p, core, 1) for v, p in zip(back, partner_rows)]
        with jax.named_scope("back_gather"):
            rows, mine, theirs = gather_both(*back)
    with jax.named_scope("gradient"):
        swaps = {}
        grad, alpha, weighted = gradient_half(
            row_at, blk_at, y_hi_pos, time_row, time_basis, rows, both_cores(mine, swaps)
        )
        swaps.update({id(v): send(after(v, alpha), CORE) for v, *_ in theirs[3:]})
        (grad,) = gradient_half(
            row_at, blk_at, 1 - y_hi_pos, time_row, time_basis, weighted, both_cores(theirs, swaps), grad
        )
    return jnp.transpose(alpha, (2, 0, 1)), grad


def solution(mesh):
    return jax.shard_map(
        per_device,
        mesh=mesh,
        in_specs=(P("space", None, "tm"), P("space", "tm"), P("tm", None), P(), P()),
        out_specs=(P("space", None, "tm"), P("space", None, "tm")),
        check_vma=False,
    )
```
